256 devices in a mesh: pair: 16 (over z, x_lo), chan: 16 (over x_hi, y, core).
Axes of the slice: x: 4 (x_hi: 2, x_lo: 2; x = x_hi * 2 + x_lo), y: 4, z: 8, core: 2. Of those that a mesh axis runs over, the one named last changes fastest.
Arguments:
- jones_start: float32 [8, 4, 128, 256], P(None, None, 'chan', 'pair'), may hold values from -4 to 4
- sky_model_products: bfloat16 [256, 8, 4, 128, 256], P('pair', None, None, 'chan'), may hold values from -6 to 6
- measured_correlations: bfloat16 [256, 8, 128, 256], P('pair', None, 'chan'), may hold values from -12 to 12
- retain_marker: int32 [256, 256], P('pair'), may hold values 0 or 1
- slot_rows: int32 [256], P('pair'), may hold values from -1 to 15, as said below
- slot_cols: int32 [256], P('pair'), may hold values from -1 to 15, as said below
Outputs:
- solutions: float32 [8, 4, 128, 256], P(None, None, 'chan', 'pair')
- duals: float32 [8, 4, 128, 256], P(None, None, 'chan', 'pair')
- consensus: float32 [8, 4, 4, 256], P(None, None, None, 'pair')
The draws below stay inside these ranges and needn't reach their ends.
Inputs may be any that keep to these rules, and one draw needn't show every extreme that they name: A live slot holds one tile of the upper triangle of 16 x 16 station blocks, slot_rows <= slot_cols; every tile is held by exactly one slot; empty slots hold -1 in both lists and follow the live slots of their device; a device holds at most 16 live slots, and some device holds exactly 16. `slot_cols`: column block of the tile in the same slot as slot_rows, -1 in empty slots.
All inputs are finite; a program needn't handle non-finite values. No bound on the sum of `retain_marker` on one device may be relied on, other than what follows from the above.
Results may differ from the reference program's by a relative error of at most 0.0003.
Values may be sent and summed in bfloat16 or wider, within the bound.
No kernel may reach another device: no remote copies, remote signals or barrier semaphores. Data moves between devices by JAX's collectives and lax.ppermute only.
A program may use at most 128 MiB of HBM per device.

```python
import math
import jax
import jax.numpy as jnp
import numpy as np
from jax import lax

STATIONS = 256
SKY_PATCHES = 4
BLK = 16
NP = 4
ITERS = 2
SPECTRAL_BINS = 128
SLOTS = 16
PLACE_SUM_ALL = 256
PATCH_PAIRINGS = 256
N_PAIR = 16


def slot_layout(key):
    blocks = STATIONS // BLK
    tiles = blocks * (blocks + 1) // 2
    upper_rows, upper_cols = np.triu_indices(blocks)
    rows_table = jnp.asarray(upper_rows, jnp.int32)
    cols_table = jnp.asarray(upper_cols, jnp.int32)
    shuffled = jax.random.permutation(jax.random.fold_in(key, 101), tiles).astype(jnp.int32)
    quarter = N_PAIR // 4
    half_axis = N_PAIR // 2
    leftover = tiles - quarter * SLOTS
    even_share = leftover // half_axis
    surplus = leftover % half_axis
    ranking = jnp.arange(N_PAIR, dtype=jnp.int32)
    pattern = jnp.where(ranking < quarter, SLOTS, jnp.where(ranking < 2 * quarter, 0, even_share + (ranking - 2 * quarter < surplus).astype(jnp.int32)))
    placing = jax.random.permutation(jax.random.fold_in(key, 102), N_PAIR).astype(jnp.int32)
    counts = pattern[placing]
    start_offsets = jnp.cumsum(counts) - counts
    slot_pos = jnp.arange(SLOTS, dtype=jnp.int32)
    occupied = slot_pos[None, :] < counts[:, None]
    position = jnp.minimum(start_offsets[:, None] + slot_pos[None, :], tiles - 1)
    chosen = shuffled[position]
    rows = jnp.where(occupied, rows_table[chosen], -1)
    cols = jnp.where(occupied, cols_table[chosen], -1)
    return (rows.reshape(-1).astype(jnp.int32), cols.reshape(-1).astype(jnp.int32))


def draw_slot_rows(key, part):
    shared = slot_layout(key)
    return shared[0]


def draw_slot_cols(key, part):
    shared = slot_layout(key)
    return shared[1]


def with_ends(array, own_key, least, high):
    longest = array.shape.index(max(array.shape))
    spots = []
    for shift in (0, 1):
        where = [jax.random.randint(jax.random.fold_in(own_key, axis), (), 0, length) for axis, length in enumerate(array.shape)]
        where[longest] = (where[longest] + shift) % array.shape[longest]
        spots.append(tuple(where))
    return array.at[spots[0]].set(least).at[spots[1]].set(high)


def levels(own_key, extent, cuts, low, high):
    def one(dim, parts):
        draws = jax.random.uniform(jax.random.fold_in(jax.random.fold_in(own_key, 6), dim), (parts,), jnp.float32, low / len(cuts), high / len(cuts))
        return jnp.repeat(jnp.exp(draws), extent[dim] // parts).reshape((-1,) + (1,) * (len(extent) - dim - 1))

    gain = one(*cuts[0])
    for cut in cuts[1:]:
        gain = gain * one(*cut)
    return gain


def scatter_about(rng, dims, deviation, bound, split=(), kind=jnp.bfloat16):
    result = jax.random.normal(rng, dims, jnp.float32) * deviation
    if len(split) > 0:
        result = levels(rng, dims, split, -0.22, 0.18) * result
    return jnp.clip(result, min=-bound, max=bound).astype(kind)


def setup_inputs(seed: int = 0) -> dict:
    key_list = jax.random.split(jax.random.key(seed), 7)
    jones_start = scatter_about(key_list[0], (8, SKY_PATCHES, SPECTRAL_BINS, STATIONS), 0.6, 4.0, ((2, 16), (3, 16)), jnp.float32)
    sky_model_products = scatter_about(key_list[1], (PLACE_SUM_ALL, 8, SKY_PATCHES, SPECTRAL_BINS, PATCH_PAIRINGS), 1.0, 6.0, ((0, 16), (3, 16)))
    measured_correlations = scatter_about(key_list[2], (PLACE_SUM_ALL, 8, SPECTRAL_BINS, PATCH_PAIRINGS), 2.0, 12.0, ((0, 16), (2, 16)))
    retain_marker = with_ends((jax.random.randint(key_list[3], (PLACE_SUM_ALL, PATCH_PAIRINGS), 0, 10) < 9).astype(jnp.int32), jax.random.fold_in(key_list[3], 1), 0, 1)
    slot_rows = draw_slot_rows(jax.random.fold_in(key_list[6], 71), 0)
    slot_cols = draw_slot_cols(jax.random.fold_in(key_list[6], 71), 0)
    return dict(jones_start=jones_start, sky_model_products=sky_model_products, measured_correlations=measured_correlations, retain_marker=retain_marker, slot_rows=slot_rows, slot_cols=slot_cols)


RHO = 0.5
MU = 1.0

def entries(matrix):
    return [(matrix[2 * e], matrix[2 * e + 1]) for e in range(4)]

def stack_entries(items):
    return jnp.stack([piece for item in items for piece in item])

def cplx_mul(left, right):
    return (left[0] * right[0] - left[1] * right[1], left[0] * right[1] + left[1] * right[0])

def cplx_add(left, right):
    return (left[0] + right[0], left[1] + right[1])

def jones_mul(left, right):
    return [cplx_add(cplx_mul(left[0], right[0]), cplx_mul(left[1], right[2])), cplx_add(cplx_mul(left[0], right[1]), cplx_mul(left[1], right[3])), cplx_add(cplx_mul(left[2], right[0]), cplx_mul(left[3], right[2])), cplx_add(cplx_mul(left[2], right[1]), cplx_mul(left[3], right[3]))]

def hermitian(matrix):
    return [(matrix[0][0], -matrix[0][1]), (matrix[2][0], -matrix[2][1]), (matrix[1][0], -matrix[1][1]), (matrix[3][0], -matrix[3][1])]

def tile_keep(flag_row, row_block, col_block, blk):
    upper = (jnp.arange(blk)[:, None] < jnp.arange(blk)[None, :]).astype(jnp.float32)
    kept = flag_row.astype(jnp.float32).reshape(blk, blk)
    return kept * jnp.where(row_block == col_block, upper, jnp.ones_like(upper))

def tile_descent(row_jones, col_jones, coher, observed, keep_mask):
    blk = row_jones.shape[-1]
    dirs = coher.shape[1]
    chans = coher.shape[2]
    coher_full = entries(coher.astype(jnp.float32).reshape(8, dirs, chans, blk, blk))
    vis_full = entries(observed.astype(jnp.float32).reshape(8, chans, blk, blk))
    left_jones = entries(row_jones[..., :, None])
    right_jones = entries(col_jones[..., None, :])
    left_coh = jones_mul(left_jones, coher_full)
    predicted = jones_mul(left_coh, hermitian(right_jones))
    residual = [((seen[0] - lax.optimization_barrier(jnp.sum(model[0], axis=0))) * keep_mask, (seen[1] - lax.optimization_barrier(jnp.sum(model[1], axis=0))) * keep_mask) for seen, model in zip(vis_full, predicted)]
    res_dirs = [(item[0][None], item[1][None]) for item in residual]
    row_terms = jones_mul(res_dirs, jones_mul(right_jones, hermitian(coher_full)))
    col_terms = jones_mul(hermitian(res_dirs), left_coh)
    row_part = stack_entries([(lax.optimization_barrier(jnp.sum(item[0], axis=-1)), lax.optimization_barrier(jnp.sum(item[1], axis=-1))) for item in row_terms])
    col_part = stack_entries([(lax.optimization_barrier(jnp.sum(item[0], axis=-2)), lax.optimization_barrier(jnp.sum(item[1], axis=-2))) for item in col_terms])
    return (row_part, col_part)

def accumulate_terms(descent, row_part, col_part, row_block, col_block, blk):
    row_start = (row_block * blk).astype(jnp.int32)
    current = lax.dynamic_slice_in_dim(descent, row_start, blk, 3)
    descent = lax.dynamic_update_slice_in_dim(descent, current + row_part, row_start, 3)
    col_start = (col_block * blk).astype(jnp.int32)
    current = lax.dynamic_slice_in_dim(descent, col_start, blk, 3)
    return lax.dynamic_update_slice_in_dim(descent, current + col_part, col_start, 3)

def poly_basis(total, first, count, terms):
    freqs = (first + jnp.arange(count)).astype(jnp.float32)
    orders = jnp.arange(terms)[:, None].astype(jnp.float32)
    waves = math.sqrt(2.0 / total) * jnp.cos(math.pi * orders * (freqs[None, :] + 0.5) / total)
    return jnp.where(orders == 0.0, math.sqrt(1.0 / total) * jnp.ones_like(waves), waves)

def project(field, basis):
    return jnp.einsum('mf,ckfs->ckms', basis, field, precision=lax.Precision.HIGHEST)

def expand(coeffs, basis):
    return jnp.einsum('mf,ckms->ckfs', basis, coeffs, precision=lax.Precision.HIGHEST)

def all_descent(jones_now, sky_model_products, measured_correlations, retain_marker, slot_rows, slot_cols):

    def one_slot(descent, slot):
        coher, observed, flag_row, row_block, col_block = slot
        occupied = (row_block >= 0).astype(jnp.float32)
        row_safe = jnp.maximum(row_block, 0)
        col_safe = jnp.maximum(col_block, 0)
        keep_mask = tile_keep(flag_row, row_safe, col_safe, BLK) * occupied
        row_jones = lax.dynamic_slice_in_dim(jones_now, (row_safe * BLK).astype(jnp.int32), BLK, 3)
        col_jones = lax.dynamic_slice_in_dim(jones_now, (col_safe * BLK).astype(jnp.int32), BLK, 3)
        row_part, col_part = tile_descent(row_jones, col_jones, coher, observed, keep_mask)
        return (accumulate_terms(descent, row_part, col_part, row_safe, col_safe, BLK), None)
    start = jnp.zeros(jones_now.shape, jnp.float32)
    descent, unused = lax.scan(one_slot, start, (sky_model_products, measured_correlations, retain_marker, slot_rows, slot_cols))
    return descent

def reference(jones_start, sky_model_products, measured_correlations, retain_marker, slot_rows, slot_cols):
    basis = poly_basis(SPECTRAL_BINS, 0, SPECTRAL_BINS, NP)
    jones_now = jones_start
    dual_now = jnp.zeros(jones_start.shape, jnp.float32)
    coeffs = project(jones_now, basis)
    for iteration in range(ITERS):
        descent = all_descent(jones_now, sky_model_products, measured_correlations, retain_marker, slot_rows, slot_cols)
        jones_now = jones_now + MU * (descent / STATIONS - dual_now - RHO * (jones_now - expand(coeffs, basis)))
        coeffs = project(jones_now + dual_now / RHO, basis)
        dual_now = dual_now + RHO * (jones_now - expand(coeffs, basis))
    return (jones_now, dual_now, coeffs)
```

```python
import math

import jax
import jax.numpy as jnp
from jax import lax
from jax.experimental import pallas as pl
from jax.experimental.pallas import tpu as pltpu
from jax.sharding import PartitionSpec as P

STATIONS = 256
BLK = 16
NP = 4
RHO = 0.5
MU = 1.0
LANES = 128
CHANS = 8
DIRS = 4
VMEM_LIMIT = 40 * 1024 * 1024


def lane_iota():
    return lax.broadcasted_iota(jnp.int32, (CHANS, LANES), 1)


def pick(vec, index):
    return jnp.take_along_axis(vec, index, axis=1, mode="promise_in_bounds")


def basis_rows(chan, total):
    freq = (chan * CHANS + lax.broadcasted_iota(jnp.int32, (CHANS, LANES), 0)).astype(jnp.float32)
    rows = [jnp.full((CHANS, LANES), math.sqrt(1.0 / total), jnp.float32)]
    for m in range(1, NP):
        rows.append(math.sqrt(2.0 / total) * jnp.cos((math.pi * m) * (freq + 0.5) / total))
    return rows


def project_rows(field, basis):
    return [jnp.sum(basis[m] * field, axis=0, keepdims=True) for m in range(NP)]


def expand_rows(coeffs, basis):
    total = basis[0] * coeffs[0:1]
    for m in range(1, NP):
        total = total + basis[m] * coeffs[m : m + 1]
    return total


def acc_mul(acc, a, b, conj_a=False, conj_b=False, minus=False):
    rr, ii = a[0] * b[0], a[1] * b[1]
    ri, ir = a[0] * b[1], a[1] * b[0]
    sign_ii = -1 if conj_a == conj_b else 1
    sign_ri = -1 if conj_b else 1
    sign_ir = -1 if conj_a else 1
    if minus:
        sign_ii, sign_ri, sign_ir = -sign_ii, -sign_ri, -sign_ir
    sign_rr = -1 if minus else 1

    def put(base, value, sign):
        if base is None:
            return value if sign > 0 else -value
        return base + value if sign > 0 else base - value

    if acc is None:
        real = rr + ii if sign_ii == sign_rr else rr - ii
        if sign_ri == sign_ir:
            imag = ri + ir
        else:
            imag = ri - ir if sign_ri > 0 else ir - ri
        if minus:
            raise ValueError
        return (real, imag)
    return (
        put(put(acc[0], rr, sign_rr), ii, sign_ii),
        put(put(acc[1], ri, sign_ri), ir, sign_ir),
    )


def mat_mul(x, y, acc=None, x_herm=False, y_herm=False, minus=False):
    out = []
    for i in range(2):
        for j in range(2):
            item = None if acc is None else acc[2 * i + j]
            for l in range(2):
                left = x[2 * l + i] if x_herm else x[2 * i + l]
                right = y[2 * j + l] if y_herm else y[2 * l + j]
                item = acc_mul(item, left, right, x_herm, y_herm, minus)
            out.append(item)
    return out


def merge(vectors, dist, lane):
    low = (lane & dist) == 0
    swap = lane ^ dist
    out = []
    for first, second in zip(vectors[0::2], vectors[1::2]):
        kept = jnp.where(low, first, second)
        sent = jnp.where(low, second, first)
        out.append(kept + pick(sent, swap))
    return out


def pairs(list8):
    return [(list8[2 * e], list8[2 * e + 1]) for e in range(4)]


def flat(matrix):
    return [piece for item in matrix for piece in item]


def descent_kernel(rows_ref, cols_ref, jones_ref, coher_ref, seen_ref, marker_ref, out_ref, left_ref, res_ref):
    lane = lane_iota()
    u_lane = lane // BLK
    v_lane = lane % BLK
    out_ref[...] = jnp.zeros_like(out_ref)

    def coher_of(t, k, half):
        kk, odd = k // 2, k % 2
        parts = []
        for e in range(8):
            block = coher_ref[t, e, 16 * kk : 16 * kk + 16, LANES * half : LANES * half + LANES]
            parts.append(block.astype(jnp.float32)[8 * odd : 8 * odd + 8])
        return pairs(parts)

    def expand(block, k, base):
        vec = jones_ref[block, k]
        return pairs([pick(vec, base + e * BLK) for e in range(8)])

    def slot(t, carry):
        a = rows_ref[t]
        b = cols_ref[t]

        @pl.when(a >= 0)
        def _():
            for half in range(2):
                acc = []
                for e in range(4):
                    both = seen_ref[
                        t, 16 * e : 16 * e + 16, LANES * half : LANES * half + LANES
                    ].astype(jnp.float32)
                    acc.append((both[0:8], both[8:16]))
                for k in range(DIRS):
                    coher = coher_of(t, k, half)
                    left = mat_mul(expand(a, k, u_lane + 8 * half), coher)
                    for e, piece in enumerate(flat(left)):
                        left_ref[half, k, e] = piece
                    acc = mat_mul(left, expand(b, k, v_lane), acc, y_herm=True, minus=True)
                mark = marker_ref[t, :, LANES * half : LANES * half + LANES]
                keep = jnp.broadcast_to(mark.astype(jnp.float32), (CHANS, LANES))
                keep = jnp.where((a != b) | (u_lane + 8 * half < v_lane), keep, 0.0)
                for e, piece in enumerate(flat(acc)):
                    res_ref[half, e] = piece * keep
            for k in range(DIRS):
                right = expand(b, k, v_lane)
                row_list = []
                col_list = None
                for half in range(2):
                    res = pairs([res_ref[half, e] for e in range(8)])
                    coher = coher_of(t, k, half)
                    turned = mat_mul(coher, right, y_herm=True)
                    row_list += flat(mat_mul(res, turned, y_herm=True))
                    left = pairs([left_ref[half, k, e] for e in range(8)])
                    if half == 0:
                        col_list = mat_mul(res, left, x_herm=True)
                    else:
                        col_list = mat_mul(res, left, col_list, x_herm=True)
                for dist in (8, 4, 2, 1):
                    row_list = merge(row_list, dist, lane)
                cols = flat(col_list)
                for dist in (64, 32, 16):
                    cols = merge(cols, dist, lane)
                s = lane % BLK
                e = lane // BLK
                j = 8 * (s // 8) + e
                place = (j & 1) * 8 + ((j >> 1) & 1) * 4 + ((j >> 2) & 1) * 2 + ((j >> 3) & 1)
                row_sum = pick(row_list[0], (s % 8) * BLK + place)
                e_back = (e & 1) * 4 + (e & 2) + (e >> 2)
                col_sum = pick(cols[0], e_back * BLK + s)
                out_ref[a, k] = out_ref[a, k] + row_sum
                out_ref[b, k] = out_ref[b, k] + col_sum

        return carry

    lax.fori_loop(0, rows_ref.shape[0], slot, 0)


def local_descent(jones_full, coher, seen, marker, rows, cols):
    blocks = jones_full.shape[0]
    vmem = pl.BlockSpec(memory_space=pltpu.VMEM)
    smem = pl.BlockSpec(memory_space=pltpu.SMEM)
    return pl.pallas_call(
        descent_kernel,
        out_shape=jax.ShapeDtypeStruct((blocks, DIRS, CHANS, LANES), jnp.float32),
        in_specs=[smem, smem, vmem, vmem, vmem, vmem],
        out_specs=vmem,
        scratch_shapes=[
            pltpu.VMEM((2, DIRS, 8, CHANS, LANES), jnp.float32),
            pltpu.VMEM((2, 8, CHANS, LANES), jnp.float32),
        ],
        compiler_params=pltpu.CompilerParams(vmem_limit_bytes=VMEM_LIMIT),
        cost_estimate=pl.CostEstimate(
            flops=40_000_000, bytes_accessed=4_000_000, transcendentals=0
        ),
    )(rows, cols, jones_full, coher, seen, marker)


def to_dense_kernel(total, chan_ref, start_ref, sent_ref, part_ref):
    basis = basis_rows(chan_ref[0], total)
    for k in range(DIRS):
        field = jnp.concatenate([start_ref[e, k] for e in range(8)], axis=1)
        for n in range(sent_ref.shape[0]):
            sent_ref[n, k] = field
        part_ref[k] = jnp.concatenate(project_rows(field, basis), axis=0)


def descent_sum(terms_ref, k):
    parts = [terms_ref[n, k] for n in range(terms_ref.shape[0])]
    while len(parts) > 1:
        parts = [x + y for x, y in zip(parts[0::2], parts[1::2])]
    return parts[0]


def first_update_kernel(total, chan_ref, jones_ref, terms_ref, *refs):
    coeff_refs, (sent_ref, part_ref) = refs[:-2], refs[-2:]
    basis = basis_rows(chan_ref[0], total)
    for k in range(DIRS):
        coeffs = coeff_refs[0][k]
        for ref in coeff_refs[1:]:
            coeffs = coeffs + ref[k]
        now = jones_ref[0, k]
        now = now + MU * (
            descent_sum(terms_ref, k) / STATIONS - RHO * (now - expand_rows(coeffs, basis))
        )
        for n in range(sent_ref.shape[0]):
            sent_ref[n, k] = now
        part_ref[k] = jnp.concatenate(project_rows(now, basis), axis=0)


def second_sum_kernel(total, chan_ref, terms_ref, part_ref, descent_ref, sent_ref):
    basis = basis_rows(chan_ref[0], total)
    for k in range(DIRS):
        descent = descent_sum(terms_ref, k)
        descent_ref[k] = descent
        part = jnp.concatenate(
            [part_ref[k], jnp.concatenate(project_rows(descent, basis), axis=0)], axis=0
        )
        for n in range(sent_ref.shape[0]):
            sent_ref[n, k] = part


def finish_kernel(total, chan_ref, jones_ref, descent_ref, sums_ref, sol_ref, du_ref, co_ref):
    basis = basis_rows(chan_ref[0], total)
    for k in range(DIRS):
        both = descent_sum(sums_ref, k)
        coeffs = both[0:NP]
        now = jones_ref[0, k]
        dual = RHO * (now - expand_rows(coeffs, basis))
        now = now + MU * (descent_ref[k] / STATIONS - dual - dual)
        coeffs = coeffs + (MU / STATIONS) * both[NP : 2 * NP]
        dual = dual + RHO * (now - expand_rows(coeffs, basis))
        for e in range(8):
            part = slice(e * BLK, e * BLK + BLK)
            sol_ref[e, k] = now[:, part]
            du_ref[e, k] = dual[:, part]
            co_ref[e, k] = coeffs[:, part]


def small_call(kernel, total, chan, arrays, shapes):
    vmem = pl.BlockSpec(memory_space=pltpu.VMEM)
    smem = pl.BlockSpec(memory_space=pltpu.SMEM)

    def body(*refs):
        kernel(total, *refs)

    return pl.pallas_call(
        body,
        out_shape=[jax.ShapeDtypeStruct(s, jnp.float32) for s in shapes],
        in_specs=[smem] + [vmem] * len(arrays),
        out_specs=[vmem] * len(shapes),
    )(chan, *arrays)


def flipped(array, bits, count):
    return lax.ppermute(array, "chan", [(i, i ^ bits) for i in range(count)])


def chan_sum_parts(part, count):
    parts = [part]
    bits = [1 << i for i in range(count.bit_length() - 1)]
    order = [bits[0], bits[-1]] + bits[1:-1]
    for i in range(0, len(order), 2):
        total = sum(parts[1:], parts[0])
        chosen = order[i : i + 2]
        masks = chosen + ([chosen[0] | chosen[1]] if len(chosen) == 2 else [])
        parts = [total] + [flipped(total, m, count) for m in masks]
    return parts


def local(start, coher, seen, marker, rows, cols):
    pair_count = lax.axis_size("pair")
    chan_count = lax.axis_size("chan")
    total = CHANS * chan_count
    chan = lax.axis_index("chan").astype(jnp.int32).reshape(1)
    coher = coher.reshape(coher.shape[0], 8, DIRS * CHANS, BLK * BLK)
    seen = seen.reshape(seen.shape[0], 8 * CHANS, BLK * BLK)
    marker = marker.reshape(marker.shape[0], 1, BLK * BLK)
    block = (DIRS, CHANS, LANES)
    blocks = (pair_count,) + block
    poly = (DIRS, NP, LANES)
    sent, part = small_call(to_dense_kernel, total, chan, [start], [blocks, poly])
    full = lax.all_to_all(sent, "pair", 0, 0)
    coeff_parts = chan_sum_parts(part, chan_count)
    terms = local_descent(full, coher, seen, marker, rows, cols)
    terms = lax.all_to_all(terms, "pair", 0, 0)
    sent, part = small_call(
        first_update_kernel, total, chan, [sent, terms] + coeff_parts, [blocks, poly]
    )
    full = lax.all_to_all(sent, "pair", 0, 0)
    terms = local_descent(full, coher, seen, marker, rows, cols)
    terms = lax.all_to_all(terms, "pair", 0, 0)
    descent, sums = small_call(
        second_sum_kernel,
        total,
        chan,
        [terms, part],
        [block, (chan_count, DIRS, 2 * NP, LANES)],
    )
    sums = lax.all_to_all(sums, "chan", 0, 0)
    return small_call(
        finish_kernel,
        total,
        chan,
        [sent, descent, sums],
        [(8, DIRS, CHANS, BLK), (8, DIRS, CHANS, BLK), (8, DIRS, NP, BLK)],
    )


def solution(mesh):
    placed = (
        P(None, None, "chan", "pair"),
        P("pair", None, None, "chan", None),
        P("pair", None, "chan", None),
        P("pair", None),
        P("pair"),
        P("pair"),
    )
    return jax.shard_map(
        local,
        mesh=mesh,
        in_specs=placed,
        out_specs=(
            P(None, None, "chan", "pair"),
            P(None, None, "chan", "pair"),
            P(None, None, None, "pair"),
        ),
        check_vma=False,
    )
```

```python
import math

import jax
import jax.numpy as jnp
from jax import lax
from jax.experimental import pallas as pl
from jax.experimental.pallas import tpu as pltpu
from jax.sharding import PartitionSpec as P

STATIONS = 256
BLK = 16
NP = 4
RHO = 0.5
MU = 1.0
LANES = 128
CHANS = 8
DIRS = 4
VMEM_LIMIT = 32 * 1024 * 1024


def lane_iota():
    return lax.broadcasted_iota(jnp.int32, (CHANS, LANES), 1)


def basis_rows(chan, total):
    freq = (chan * CHANS + lax.broadcasted_iota(jnp.int32, (CHANS, LANES), 0)).astype(jnp.float32)
    rows = [jnp.full((CHANS, LANES), math.sqrt(1.0 / total), jnp.float32)]
    for m in range(1, NP):
        rows.append(math.sqrt(2.0 / total) * jnp.cos((math.pi * m) * (freq + 0.5) / total))
    return rows


def project_rows(field, basis):
    return [jnp.sum(basis[m] * field, axis=0, keepdims=True) for m in range(NP)]


def expand_rows(coeffs, basis):
    total = basis[0] * coeffs[0:1]
    for m in range(1, NP):
        total = total + basis[m] * coeffs[m : m + 1]
    return total


def acc_mul(acc, a, b, conj_a=False, conj_b=False, minus=False):
    rr, ii = a[0] * b[0], a[1] * b[1]
    ri, ir = a[0] * b[1], a[1] * b[0]
    sign_ii = -1 if conj_a == conj_b else 1
    sign_ri = -1 if conj_b else 1
    sign_ir = -1 if conj_a else 1
    if minus:
        sign_ii, sign_ri, sign_ir = -sign_ii, -sign_ri, -sign_ir
    sign_rr = -1 if minus else 1

    def put(base, value, sign):
        if base is None:
            return value if sign > 0 else -value
        return base + value if sign > 0 else base - value

    if acc is None:
        real = rr + ii if sign_ii == sign_rr else rr - ii
        if sign_ri == sign_ir:
            imag = ri + ir
        else:
            imag = ri - ir if sign_ri > 0 else ir - ri
        if minus:
            raise ValueError
        return (real, imag)
    return (
        put(put(acc[0], rr, sign_rr), ii, sign_ii),
        put(put(acc[1], ri, sign_ri), ir, sign_ir),
    )


def mat_mul(x, y, acc=None, x_herm=False, y_herm=False, minus=False):
    out = []
    for i in range(2):
        for j in range(2):
            item = None if acc is None else acc[2 * i + j]
            for l in range(2):
                left = x[2 * l + i] if x_herm else x[2 * i + l]
                right = y[2 * j + l] if y_herm else y[2 * l + j]
                item = acc_mul(item, left, right, x_herm, y_herm, minus)
            out.append(item)
    return out


def mat_entry(x, y, i, j, item=None, x_herm=False, y_herm=False):
    for l in range(2):
        left = x[2 * l + i] if x_herm else x[2 * i + l]
        right = y[2 * j + l] if y_herm else y[2 * l + j]
        item = acc_mul(item, left, right, x_herm, y_herm)
    return item


def pairs(list8):
    return [(list8[2 * e], list8[2 * e + 1]) for e in range(4)]


def flat(matrix):
    return [piece for item in matrix for piece in item]


def one_hot(hit):
    return jnp.where(hit, 1.0, 0.0).astype(jnp.bfloat16)


def stage_kernel(rows_ref, cols_ref, marker_ref, keep_ref, spread_ref, sums_ref):
    source = lax.broadcasted_iota(jnp.int32, (LANES, LANES), 0)
    target = lax.broadcasted_iota(jnp.int32, (LANES, LANES), 1)
    tables = [target % BLK, target // BLK, target // BLK + 8]
    for n in range(24):
        one = one_hot(source == (n // 3) * BLK + tables[n % 3])
        spread_ref[0:LANES, n * LANES : n * LANES + LANES] = one
        spread_ref[LANES : 2 * LANES, n * LANES : n * LANES + LANES] = one
    for n in range(4):
        sums_ref[0, n * LANES : n * LANES + LANES] = one_hot(target == 2 * n * BLK + source // BLK)
        sums_ref[1, n * LANES : n * LANES + LANES] = one_hot(target == 2 * n * BLK + source % BLK)

    lane = lane_iota()
    for t in range(rows_ref.shape[0]):
        for half in range(2):
            mark = marker_ref[t : t + 1, LANES * half : LANES * half + LANES].astype(jnp.float32)
            keep = jnp.broadcast_to(mark, (CHANS, LANES))
            off_diagonal = rows_ref[t] != cols_ref[t]
            upper = lane // BLK + 8 * half < lane % BLK
            keep = jnp.where((off_diagonal | upper) & (rows_ref[t] >= 0), keep, 0.0)
            keep_ref[t, half] = keep


def stage(marker, rows, cols):
    slots = rows.shape[0]
    vmem = pl.BlockSpec(memory_space=pltpu.VMEM)
    smem = pl.BlockSpec(memory_space=pltpu.SMEM)
    return pl.pallas_call(
        stage_kernel,
        out_shape=[
            pltpu.VMEM((slots, 2, CHANS, LANES), jnp.float32),
            pltpu.VMEM((2 * LANES, 24 * LANES), jnp.bfloat16),
            pltpu.VMEM((2, 4 * LANES, LANES), jnp.bfloat16),
        ],
        in_specs=[smem, smem, vmem],
        out_specs=[vmem] * 3,
        cost_estimate=pl.CostEstimate(flops=1_000_000, bytes_accessed=2_000_000, transcendentals=0),
    )(rows, cols, marker)


def descent_kernel(
    rows_ref, cols_ref, jones_ref, coher_hbm, seen_hbm, keep_ref, spread_ref, sums_ref, *refs
):
    outer, scratch = refs[:-9], refs[-9:]
    if len(outer) > 1:
        part_refs, (out_ref, sum_ref) = outer[:-2], outer[-2:]
        sum_ref[...] = sum([ref[...] for ref in part_refs[1:]], part_refs[0][...])
    else:
        (out_ref,) = outer
    coher_ref, seen_ref, wide_ref, left_ref, res_ref, row_ref, col_ref, coher_sem, seen_sem = scratch
    slots = rows_ref.shape[0]
    blocks = jones_ref.shape[0]

    def copies(t):
        return (
            pltpu.make_async_copy(coher_hbm.at[t], coher_ref.at[t], coher_sem.at[t]),
            pltpu.make_async_copy(seen_hbm.at[t], seen_ref.at[t], seen_sem.at[t]),
        )

    for t in range(slots):
        for copy in copies(t):
            copy.start()
    out_ref[...] = jnp.zeros_like(out_ref)

    dense = jones_ref[...].reshape(blocks * DIRS * CHANS, LANES)
    high = dense.astype(jnp.bfloat16)
    low = (dense - high.astype(jnp.float32)).astype(jnp.bfloat16)
    split = jnp.concatenate([high, low], axis=1)
    for c in range(12):
        part = slice(256 * c, 256 * c + 256)
        wide = jnp.dot(split, spread_ref[:, part], preferred_element_type=jnp.float32)
        wide_ref[:, :, part] = wide.reshape(blocks * DIRS, CHANS, 256)

    def coher_of(t, k, half):
        kk, odd = k // 2, k % 2
        parts = []
        for e in range(8):
            block = coher_ref[t, e, 16 * kk : 16 * kk + 16, LANES * half : LANES * half + LANES]
            parts.append(block.astype(jnp.float32)[8 * odd : 8 * odd + 8])
        return pairs(parts)

    def expand(block, k, kind):
        return pairs(
            [
                wide_ref[block * DIRS + k, :, (3 * e + kind) * LANES : (3 * e + kind + 1) * LANES]
                for e in range(8)
            ]
        )

    def put(ref, part, item):
        ref[0:8, part * LANES : part * LANES + LANES] = item[0]
        ref[8:16, part * LANES : part * LANES + LANES] = item[1]

    def multiply(t, carry):
        a = jnp.maximum(rows_ref[t], 0)
        b = jnp.maximum(cols_ref[t], 0)
        for copy in copies(t):
            copy.wait()
        for half in range(2):
            acc = []
            for e in range(4):
                both = seen_ref[
                    t, 16 * e : 16 * e + 16, LANES * half : LANES * half + LANES
                ].astype(jnp.float32)
                acc.append((both[0:8], both[8:16]))
            for k in range(DIRS):
                left = mat_mul(expand(a, k, 1 + half), coher_of(t, k, half))
                for e, piece in enumerate(flat(left)):
                    left_ref[half, k, e] = piece
                acc = mat_mul(left, expand(b, k, 0), acc, y_herm=True, minus=True)
            keep = keep_ref[t, half]
            for e, piece in enumerate(flat(acc)):
                res_ref[half, e] = piece * keep
        for k in range(DIRS):
            right = expand(b, k, 0)
            cols = [None] * 4
            for half in range(2):
                res = pairs([res_ref[half, e] for e in range(8)])
                turned = mat_mul(coher_of(t, k, half), right, y_herm=True)
                for e in range(4):
                    item = mat_entry(res, turned, e // 2, e % 2, y_herm=True)
                    put(row_ref.at[t, k, half], e, item)
                left = pairs([left_ref[half, k, e] for e in range(8)])
                for e in range(4):
                    cols[e] = mat_entry(res, left, e // 2, e % 2, cols[e], x_herm=True)
                    if half == 1:
                        put(col_ref.at[t, k], e, cols[e])
        return carry

    lax.fori_loop(0, slots, multiply, 0)

    group = 8

    def total(values, sums):
        high = values.astype(jnp.bfloat16)
        low = (values - high.astype(jnp.float32)).astype(jnp.bfloat16)
        out = jnp.dot(high, sums, preferred_element_type=jnp.float32)
        return out + jnp.dot(low, sums, preferred_element_type=jnp.float32)

    def settle(g, carry):
        t0 = g * group
        rows = total(row_ref[pl.ds(t0, group)].reshape(group * DIRS * 32, 4 * LANES), sums_ref[0])
        cols = total(col_ref[pl.ds(t0, group)].reshape(group * DIRS * 16, 4 * LANES), sums_ref[1])
        rows = rows.reshape(group, DIRS, 2, 2, CHANS, LANES)
        cols = cols.reshape(group, DIRS, 2, CHANS, LANES)
        for n in range(group):
            a = jnp.maximum(rows_ref[t0 + n], 0)
            b = jnp.maximum(cols_ref[t0 + n], 0)
            for k in range(DIRS):
                row = [rows[n, k, 0, c] + pltpu.roll(rows[n, k, 1, c], 8, 1) for c in range(2)]
                row = row[0] + pltpu.roll(row[1], BLK, 1)
                out_ref[a, k] = out_ref[a, k] + row
            for k in range(DIRS):
                col = cols[n, k, 0] + pltpu.roll(cols[n, k, 1], BLK, 1)
                out_ref[b, k] = out_ref[b, k] + col
        return carry

    lax.fori_loop(0, slots // group, settle, 0)


def local_descent(jones_full, rows, cols, coher, seen, staged, parts):
    blocks = jones_full.shape[0]
    slots = rows.shape[0]
    vmem = pl.BlockSpec(memory_space=pltpu.VMEM)
    smem = pl.BlockSpec(memory_space=pltpu.SMEM)
    hbm = pl.BlockSpec(memory_space=pltpu.HBM)
    tiles = [pltpu.with_memory_space_constraint(x, pltpu.HBM) for x in (coher, seen)]
    staged = [pltpu.with_memory_space_constraint(x, pltpu.VMEM) for x in staged]
    out_shape = [jax.ShapeDtypeStruct((blocks, DIRS, CHANS, LANES), jnp.float32)]
    if len(parts) > 0:
        out_shape.append(jax.ShapeDtypeStruct(parts[0].shape, jnp.float32))
    return pl.pallas_call(
        descent_kernel,
        out_shape=out_shape,
        in_specs=[smem, smem, vmem, hbm, hbm] + [vmem] * (3 + len(parts)),
        out_specs=[vmem] * len(out_shape),
        scratch_shapes=[
            pltpu.VMEM(coher.shape, jnp.bfloat16),
            pltpu.VMEM(seen.shape, jnp.bfloat16),
            pltpu.VMEM((blocks * DIRS, CHANS, 24 * LANES), jnp.float32),
            pltpu.VMEM((2, DIRS, 8, CHANS, LANES), jnp.float32),
            pltpu.VMEM((2, 8, CHANS, LANES), jnp.float32),
            pltpu.VMEM((slots, DIRS, 2, 16, 4 * LANES), jnp.float32),
            pltpu.VMEM((slots, DIRS, 16, 4 * LANES), jnp.float32),
            pltpu.SemaphoreType.DMA((slots,)),
            pltpu.SemaphoreType.DMA((slots,)),
        ],
        compiler_params=pltpu.CompilerParams(vmem_limit_bytes=VMEM_LIMIT),
        cost_estimate=pl.CostEstimate(
            flops=40_000_000, bytes_accessed=4_000_000, transcendentals=0
        ),
    )(rows, cols, jones_full, *tiles, *staged, *parts)


def to_dense_kernel(total, chan_ref, start_ref, sent_ref, part_ref):
    basis = basis_rows(chan_ref[0], total)
    for k in range(DIRS):
        field = jnp.concatenate([start_ref[e, k] for e in range(8)], axis=1)
        for n in range(sent_ref.shape[0]):
            sent_ref[n, k] = field
        part_ref[k] = jnp.concatenate(project_rows(field, basis), axis=0)


def descent_sum(terms_ref, k):
    parts = [terms_ref[n, k] for n in range(terms_ref.shape[0])]
    while len(parts) > 1:
        parts = [x + y for x, y in zip(parts[0::2], parts[1::2])]
    return parts[0]


def first_update_kernel(total, chan_ref, jones_ref, terms_ref, *refs):
    coeff_refs, (sent_ref, part_ref) = refs[:-2], refs[-2:]
    basis = basis_rows(chan_ref[0], total)
    for k in range(DIRS):
        coeffs = coeff_refs[0][k]
        for ref in coeff_refs[1:]:
            coeffs = coeffs + ref[k]
        now = jones_ref[0, k]
        now = now + MU * (
            descent_sum(terms_ref, k) / STATIONS - RHO * (now - expand_rows(coeffs, basis))
        )
        for n in range(sent_ref.shape[0]):
            sent_ref[n, k] = now
        part_ref[k] = jnp.concatenate(project_rows(now, basis), axis=0)


def second_sum_kernel(total, chan_ref, terms_ref, part_ref, descent_ref, sent_ref):
    basis = basis_rows(chan_ref[0], total)
    for k in range(DIRS):
        descent = descent_sum(terms_ref, k)
        descent_ref[k] = descent
        part = jnp.concatenate(
            [part_ref[k], jnp.concatenate(project_rows(descent, basis), axis=0)], axis=0
        )
        for n in range(sent_ref.shape[0]):
            sent_ref[n, k] = part


def finish_kernel(total, chan_ref, jones_ref, descent_ref, sums_ref, sol_ref, du_ref, co_ref):
    basis = basis_rows(chan_ref[0], total)
    for k in range(DIRS):
        both = descent_sum(sums_ref, k)
        coeffs = both[0:NP]
        now = jones_ref[0, k]
        dual = RHO * (now - expand_rows(coeffs, basis))
        now = now + MU * (descent_ref[k] / STATIONS - dual - dual)
        coeffs = coeffs + (MU / STATIONS) * both[NP : 2 * NP]
        dual = dual + RHO * (now - expand_rows(coeffs, basis))
        for e in range(8):
            part = slice(e * BLK, e * BLK + BLK)
            sol_ref[e, k] = now[:, part]
            du_ref[e, k] = dual[:, part]
            co_ref[e, k] = coeffs[:, part]


def small_call(kernel, total, chan, arrays, shapes):
    vmem = pl.BlockSpec(memory_space=pltpu.VMEM)
    smem = pl.BlockSpec(memory_space=pltpu.SMEM)

    def body(*refs):
        kernel(total, *refs)

    return pl.pallas_call(
        body,
        out_shape=[jax.ShapeDtypeStruct(s, jnp.float32) for s in shapes],
        in_specs=[smem] + [vmem] * len(arrays),
        out_specs=[vmem] * len(shapes),
    )(chan, *arrays)


def flipped(array, bits, count):
    return lax.ppermute(array, "chan", [(i, i ^ bits) for i in range(count)])


def exchanged(part, bits, count):
    masks = [0]
    for bit in bits:
        masks += [m ^ bit for m in masks]
    return [part] + [flipped(part, m, count) for m in masks[1:]]


def local(start, coher, seen, marker, rows, cols):
    pair_count = lax.axis_size("pair")
    chan_count = lax.axis_size("chan")
    total = CHANS * chan_count
    chan = lax.axis_index("chan").astype(jnp.int32).reshape(1)
    coher = coher.reshape(coher.shape[0], 8, DIRS * CHANS, BLK * BLK)
    seen = seen.reshape(seen.shape[0], 8 * CHANS, BLK * BLK)
    staged = stage(marker, rows, cols)
    block = (DIRS, CHANS, LANES)
    blocks = (pair_count,) + block
    poly = (DIRS, NP, LANES)
    sent, part = small_call(to_dense_kernel, total, chan, [start], [blocks, poly])
    full = lax.all_to_all(sent, "pair", 0, 0)
    bits = [1 << i for i in range(chan_count.bit_length() - 1)]
    parts = exchanged(part, bits[:1] + bits[3:], chan_count)
    terms, part = local_descent(full, rows, cols, coher, seen, staged, parts)
    coeff_parts = exchanged(part, bits[1:3], chan_count)
    terms = lax.all_to_all(terms, "pair", 0, 0)
    sent, part = small_call(
        first_update_kernel, total, chan, [sent, terms] + coeff_parts, [blocks, poly]
    )
    full = lax.all_to_all(sent, "pair", 0, 0)
    (terms,) = local_descent(full, rows, cols, coher, seen, staged, [])
    terms = lax.all_to_all(terms, "pair", 0, 0)
    descent, sums = small_call(
        second_sum_kernel,
        total,
        chan,
        [terms, part],
        [block, (chan_count, DIRS, 2 * NP, LANES)],
    )
    sums = lax.all_to_all(sums, "chan", 0, 0)
    return small_call(
        finish_kernel,
        total,
        chan,
        [sent, descent, sums],
        [(8, DIRS, CHANS, BLK), (8, DIRS, CHANS, BLK), (8, DIRS, NP, BLK)],
    )


def solution(mesh):
    placed = (
        P(None, None, "chan", "pair"),
        P("pair", None, None, "chan", None),
        P("pair", None, "chan", None),
        P("pair", None),
        P("pair"),
        P("pair"),
    )
    return jax.shard_map(
        local,
        mesh=mesh,
        in_specs=placed,
        out_specs=(
            P(None, None, "chan", "pair"),
            P(None, None, "chan", "pair"),
            P(None, None, None, "pair"),
        ),
        check_vma=False,
    )
```

```python
import math

import jax
import jax.numpy as jnp
from jax import lax
from jax.experimental import pallas as pl
from jax.experimental.pallas import tpu as pltpu
from jax.sharding import PartitionSpec as P

STATIONS = 256
BLK = 16
NP = 4
RHO = 0.5
MU = 1.0
LANES = 128
CHANS = 8
DIRS = 4
VMEM_LIMIT = 32 * 1024 * 1024
SMALL_LIMIT = 8 * 1024 * 1024


def in_hbm(array):
    return pltpu.with_memory_space_constraint(array, pltpu.HBM)


def lane_iota():
    return lax.broadcasted_iota(jnp.int32, (CHANS, LANES), 1)


def basis_rows(chan, total):
    freq = (chan * CHANS + lax.broadcasted_iota(jnp.int32, (CHANS, LANES), 0)).astype(jnp.float32)
    rows = [jnp.full((CHANS, LANES), math.sqrt(1.0 / total), jnp.float32)]
    for m in range(1, NP):
        rows.append(math.sqrt(2.0 / total) * jnp.cos((math.pi * m) * (freq + 0.5) / total))
    return rows


def project_rows(field, basis):
    return [jnp.sum(basis[m] * field, axis=0, keepdims=True) for m in range(NP)]


def expand_rows(coeffs, basis):
    total = basis[0] * coeffs[0:1]
    for m in range(1, NP):
        total = total + basis[m] * coeffs[m : m + 1]
    return total


def acc_mul(acc, a, b, conj_a=False, conj_b=False, minus=False):
    rr, ii = a[0] * b[0], a[1] * b[1]
    ri, ir = a[0] * b[1], a[1] * b[0]
    sign_ii = -1 if conj_a == conj_b else 1
    sign_ri = -1 if conj_b else 1
    sign_ir = -1 if conj_a else 1
    if minus:
        sign_ii, sign_ri, sign_ir = -sign_ii, -sign_ri, -sign_ir
    sign_rr = -1 if minus else 1

    def put(base, value, sign):
        if base is None:
            return value if sign > 0 else -value
        return base + value if sign > 0 else base - value

    if acc is None:
        real = rr + ii if sign_ii == sign_rr else rr - ii
        if sign_ri == sign_ir:
            imag = ri + ir
        else:
            imag = ri - ir if sign_ri > 0 else ir - ri
        if minus:
            raise ValueError
        return (real, imag)
    return (
        put(put(acc[0], rr, sign_rr), ii, sign_ii),
        put(put(acc[1], ri, sign_ri), ir, sign_ir),
    )


def mat_mul(x, y, acc=None, x_herm=False, y_herm=False, minus=False):
    out = []
    for i in range(2):
        for j in range(2):
            item = None if acc is None else acc[2 * i + j]
            for l in range(2):
                left = x[2 * l + i] if x_herm else x[2 * i + l]
                right = y[2 * j + l] if y_herm else y[2 * l + j]
                item = acc_mul(item, left, right, x_herm, y_herm, minus)
            out.append(item)
    return out


def mat_entry(x, y, i, j, item=None, x_herm=False, y_herm=False):
    for l in range(2):
        left = x[2 * l + i] if x_herm else x[2 * i + l]
        right = y[2 * j + l] if y_herm else y[2 * l + j]
        item = acc_mul(item, left, right, x_herm, y_herm)
    return item


def pairs(list8):
    return [(list8[2 * e], list8[2 * e + 1]) for e in range(4)]


def flat(matrix):
    return [piece for item in matrix for piece in item]


def one_hot(hit):
    return jnp.where(hit, 1.0, 0.0).astype(jnp.bfloat16)


def stage_kernel(rows_ref, cols_ref, marker_ref, keep_ref, spread_ref, sums_ref):
    source = lax.broadcasted_iota(jnp.int32, (LANES, LANES), 0)
    target = lax.broadcasted_iota(jnp.int32, (LANES, LANES), 1)
    tables = [target % BLK, target // BLK, target // BLK + 8]
    for n in range(24):
        one = one_hot(source == (n // 3) * BLK + tables[n % 3])
        spread_ref[0:LANES, n * LANES : n * LANES + LANES] = one
        spread_ref[LANES : 2 * LANES, n * LANES : n * LANES + LANES] = one
    for n in range(4):
        sums_ref[0, n * LANES : n * LANES + LANES] = one_hot(target == 2 * n * BLK + source // BLK)
        sums_ref[1, n * LANES : n * LANES + LANES] = one_hot(target == 2 * n * BLK + source % BLK)

    lane = lane_iota()
    for t in range(rows_ref.shape[0]):
        for half in range(2):
            mark = marker_ref[t : t + 1, LANES * half : LANES * half + LANES].astype(jnp.float32)
            keep = jnp.broadcast_to(mark, (CHANS, LANES))
            off_diagonal = rows_ref[t] != cols_ref[t]
            upper = lane // BLK + 8 * half < lane % BLK
            keep = jnp.where((off_diagonal | upper) & (rows_ref[t] >= 0), keep, 0.0)
            keep_ref[t, half] = keep


def stage(marker, rows, cols):
    slots = rows.shape[0]
    vmem = pl.BlockSpec(memory_space=pltpu.VMEM)
    smem = pl.BlockSpec(memory_space=pltpu.SMEM)
    return pl.pallas_call(
        stage_kernel,
        out_shape=[
            pltpu.VMEM((slots, 2, CHANS, LANES), jnp.float32),
            pltpu.VMEM((2 * LANES, 24 * LANES), jnp.bfloat16),
            pltpu.VMEM((2, 4 * LANES, LANES), jnp.bfloat16),
        ],
        in_specs=[smem, smem, vmem],
        out_specs=[vmem] * 3,
        compiler_params=pltpu.CompilerParams(vmem_limit_bytes=SMALL_LIMIT),
        cost_estimate=pl.CostEstimate(flops=1_000_000, bytes_accessed=2_000_000, transcendentals=0),
    )(in_hbm(rows), in_hbm(cols), in_hbm(marker))


def descent_kernel(
    rows_ref, cols_ref, jones_ref, coher_hbm, seen_hbm, keep_ref, spread_ref, sums_ref, *refs
):
    outer, scratch = refs[:-9], refs[-9:]
    if len(outer) > 1:
        part_refs, (out_ref, sum_ref) = outer[:-2], outer[-2:]
        sum_ref[...] = sum([ref[...] for ref in part_refs[1:]], part_refs[0][...])
    else:
        (out_ref,) = outer
    coher_ref, seen_ref, wide_ref, left_ref, res_ref, row_ref, col_ref, coher_sem, seen_sem = scratch
    slots = rows_ref.shape[0]
    blocks = jones_ref.shape[0]

    def copies(t):
        return (
            pltpu.make_async_copy(coher_hbm.at[t], coher_ref.at[t], coher_sem.at[t]),
            pltpu.make_async_copy(seen_hbm.at[t], seen_ref.at[t], seen_sem.at[t]),
        )

    for t in range(slots):
        for copy in copies(t):
            copy.start()
    out_ref[...] = jnp.zeros_like(out_ref)

    dense = jones_ref[...].reshape(blocks * DIRS * CHANS, LANES)
    high = dense.astype(jnp.bfloat16)
    low = (dense - high.astype(jnp.float32)).astype(jnp.bfloat16)
    split = jnp.concatenate([high, low], axis=1)
    for c in range(12):
        part = slice(256 * c, 256 * c + 256)
        wide = jnp.dot(split, spread_ref[:, part], preferred_element_type=jnp.float32)
        wide_ref[:, :, part] = wide.reshape(blocks * DIRS, CHANS, 256)

    def coher_of(t, k, half):
        kk, odd = k // 2, k % 2
        parts = []
        for e in range(8):
            block = coher_ref[t, e, 16 * kk : 16 * kk + 16, LANES * half : LANES * half + LANES]
            parts.append(block.astype(jnp.float32)[8 * odd : 8 * odd + 8])
        return pairs(parts)

    def expand(block, k, kind):
        return pairs(
            [
                wide_ref[block * DIRS + k, :, (3 * e + kind) * LANES : (3 * e + kind + 1) * LANES]
                for e in range(8)
            ]
        )

    def put(ref, part, item):
        ref[0:8, part * LANES : part * LANES + LANES] = item[0]
        ref[8:16, part * LANES : part * LANES + LANES] = item[1]

    def multiply(t, carry):
        a = jnp.maximum(rows_ref[t], 0)
        b = jnp.maximum(cols_ref[t], 0)
        for copy in copies(t):
            copy.wait()
        for half in range(2):
            acc = []
            for e in range(4):
                both = seen_ref[
                    t, 16 * e : 16 * e + 16, LANES * half : LANES * half + LANES
                ].astype(jnp.float32)
                acc.append((both[0:8], both[8:16]))
            for k in range(DIRS):
                left = mat_mul(expand(a, k, 1 + half), coher_of(t, k, half))
                for e, piece in enumerate(flat(left)):
                    left_ref[half, k, e] = piece
                acc = mat_mul(left, expand(b, k, 0), acc, y_herm=True, minus=True)
            keep = keep_ref[t, half]
            for e, piece in enumerate(flat(acc)):
                res_ref[half, e] = piece * keep
        for k in range(DIRS):
            right = expand(b, k, 0)
            cols = [None] * 4
            for half in range(2):
                res = pairs([res_ref[half, e] for e in range(8)])
                turned = mat_mul(coher_of(t, k, half), right, y_herm=True)
                for e in range(4):
                    item = mat_entry(res, turned, e // 2, e % 2, y_herm=True)
                    put(row_ref.at[t, k, half], e, item)
                left = pairs([left_ref[half, k, e] for e in range(8)])
                for e in range(4):
                    cols[e] = mat_entry(res, left, e // 2, e % 2, cols[e], x_herm=True)
                    if half == 1:
                        put(col_ref.at[t, k], e, cols[e])
        return carry

    lax.fori_loop(0, slots, multiply, 0)

    group = 8

    def total(values, sums):
        high = values.astype(jnp.bfloat16)
        low = (values - high.astype(jnp.float32)).astype(jnp.bfloat16)
        out = jnp.dot(high, sums, preferred_element_type=jnp.float32)
        return out + jnp.dot(low, sums, preferred_element_type=jnp.float32)

    def settle(g, carry):
        t0 = g * group
        rows = total(row_ref[pl.ds(t0, group)].reshape(group * DIRS * 32, 4 * LANES), sums_ref[0])
        cols = total(col_ref[pl.ds(t0, group)].reshape(group * DIRS * 16, 4 * LANES), sums_ref[1])
        rows = rows.reshape(group, DIRS, 2, 2, CHANS, LANES)
        cols = cols.reshape(group, DIRS, 2, CHANS, LANES)
        for n in range(group):
            a = jnp.maximum(rows_ref[t0 + n], 0)
            b = jnp.maximum(cols_ref[t0 + n], 0)
            for k in range(DIRS):
                row = [rows[n, k, 0, c] + pltpu.roll(rows[n, k, 1, c], 8, 1) for c in range(2)]
                row = row[0] + pltpu.roll(row[1], BLK, 1)
                out_ref[a, k] = out_ref[a, k] + row
            for k in range(DIRS):
                col = cols[n, k, 0] + pltpu.roll(cols[n, k, 1], BLK, 1)
                out_ref[b, k] = out_ref[b, k] + col
        return carry

    lax.fori_loop(0, slots // group, settle, 0)


def local_descent(jones_full, rows, cols, coher, seen, staged, parts):
    blocks = jones_full.shape[0]
    slots = rows.shape[0]
    vmem = pl.BlockSpec(memory_space=pltpu.VMEM)
    smem = pl.BlockSpec(memory_space=pltpu.SMEM)
    hbm = pl.BlockSpec(memory_space=pltpu.HBM)
    staged = [pltpu.with_memory_space_constraint(x, pltpu.VMEM) for x in staged]
    out_shape = [jax.ShapeDtypeStruct((blocks, DIRS, CHANS, LANES), jnp.float32)]
    if len(parts) > 0:
        out_shape.append(jax.ShapeDtypeStruct(parts[0].shape, jnp.float32))
    return pl.pallas_call(
        descent_kernel,
        out_shape=out_shape,
        in_specs=[smem, smem, vmem, hbm, hbm] + [vmem] * (3 + len(parts)),
        out_specs=[vmem] * len(out_shape),
        scratch_shapes=[
            pltpu.VMEM(coher.shape, jnp.bfloat16),
            pltpu.VMEM(seen.shape, jnp.bfloat16),
            pltpu.VMEM((blocks * DIRS, CHANS, 24 * LANES), jnp.float32),
            pltpu.VMEM((2, DIRS, 8, CHANS, LANES), jnp.float32),
            pltpu.VMEM((2, 8, CHANS, LANES), jnp.float32),
            pltpu.VMEM((slots, DIRS, 2, 16, 4 * LANES), jnp.float32),
            pltpu.VMEM((slots, DIRS, 16, 4 * LANES), jnp.float32),
            pltpu.SemaphoreType.DMA((slots,)),
            pltpu.SemaphoreType.DMA((slots,)),
        ],
        compiler_params=pltpu.CompilerParams(vmem_limit_bytes=VMEM_LIMIT),
        cost_estimate=pl.CostEstimate(
            flops=40_000_000, bytes_accessed=4_000_000, transcendentals=0
        ),
    )(in_hbm(rows), in_hbm(cols), jones_full, in_hbm(coher), in_hbm(seen), *staged, *parts)


def to_dense_kernel(total, chan_ref, start_ref, sent_ref, part_ref):
    basis = basis_rows(chan_ref[0], total)
    for k in range(DIRS):
        field = jnp.concatenate([start_ref[e, k] for e in range(8)], axis=1)
        for n in range(sent_ref.shape[0]):
            sent_ref[n, k] = field
        part_ref[k] = jnp.concatenate(project_rows(field, basis), axis=0)


def descent_sum(terms_ref, k):
    parts = [terms_ref[n, k] for n in range(terms_ref.shape[0])]
    while len(parts) > 1:
        parts = [x + y for x, y in zip(parts[0::2], parts[1::2])]
    return parts[0]


def first_update_kernel(total, chan_ref, jones_ref, terms_ref, *refs):
    coeff_refs, (sent_ref, part_ref) = refs[:-2], refs[-2:]
    basis = basis_rows(chan_ref[0], total)
    for k in range(DIRS):
        coeffs = coeff_refs[0][k]
        for ref in coeff_refs[1:]:
            coeffs = coeffs + ref[k]
        now = jones_ref[0, k]
        now = now + MU * (
            descent_sum(terms_ref, k) / STATIONS - RHO * (now - expand_rows(coeffs, basis))
        )
        for n in range(sent_ref.shape[0]):
            sent_ref[n, k] = now
        part_ref[k] = jnp.concatenate(project_rows(now, basis), axis=0)


def second_sum_kernel(total, chan_ref, terms_ref, part_ref, descent_ref, sent_ref):
    basis = basis_rows(chan_ref[0], total)
    for k in range(DIRS):
        descent = descent_sum(terms_ref, k)
        descent_ref[k] = descent
        part = jnp.concatenate(
            [part_ref[k], jnp.concatenate(project_rows(descent, basis), axis=0)], axis=0
        )
        for n in range(sent_ref.shape[0]):
            sent_ref[n, k] = part


def finish_kernel(total, chan_ref, jones_ref, descent_ref, sums_ref, sol_ref, du_ref, co_ref):
    basis = basis_rows(chan_ref[0], total)
    for k in range(DIRS):
        both = descent_sum(sums_ref, k)
        coeffs = both[0:NP]
        now = jones_ref[0, k]
        dual = RHO * (now - expand_rows(coeffs, basis))
        now = now + MU * (descent_ref[k] / STATIONS - dual - dual)
        coeffs = coeffs + (MU / STATIONS) * both[NP : 2 * NP]
        dual = dual + RHO * (now - expand_rows(coeffs, basis))
        for e in range(8):
            part = slice(e * BLK, e * BLK + BLK)
            sol_ref[e, k] = now[:, part]
            du_ref[e, k] = dual[:, part]
            co_ref[e, k] = coeffs[:, part]


def small_call(kernel, total, chan, arrays, shapes):
    vmem = pl.BlockSpec(memory_space=pltpu.VMEM)
    smem = pl.BlockSpec(memory_space=pltpu.SMEM)

    def body(*refs):
        kernel(total, *refs)

    return pl.pallas_call(
        body,
        out_shape=[jax.ShapeDtypeStruct(s, jnp.float32) for s in shapes],
        in_specs=[smem] + [vmem] * len(arrays),
        out_specs=[vmem] * len(shapes),
        compiler_params=pltpu.CompilerParams(vmem_limit_bytes=SMALL_LIMIT),
    )(in_hbm(chan), *arrays)


def flipped(array, bits, count):
    return lax.ppermute(array, "chan", [(i, i ^ bits) for i in range(count)])


def exchanged(part, bits, count):
    masks = [0]
    for bit in bits:
        masks += [m ^ bit for m in masks]
    return [part] + [flipped(part, m, count) for m in masks[1:]]


def local(start, coher, seen, marker, rows, cols):
    pair_count = lax.axis_size("pair")
    chan_count = lax.axis_size("chan")
    total = CHANS * chan_count
    chan = lax.axis_index("chan").astype(jnp.int32).reshape(1)
    coher = coher.reshape(coher.shape[0], 8, DIRS * CHANS, BLK * BLK)
    seen = seen.reshape(seen.shape[0], 8 * CHANS, BLK * BLK)
    staged = stage(marker, rows, cols)
    block = (DIRS, CHANS, LANES)
    blocks = (pair_count,) + block
    poly = (DIRS, NP, LANES)
    sent, part = small_call(to_dense_kernel, total, chan, [start], [blocks, poly])
    full = lax.all_to_all(sent, "pair", 0, 0)
    bits = [1 << i for i in range(chan_count.bit_length() - 1)]
    parts = exchanged(part, bits[:1] + bits[3:], chan_count)
    terms, part = local_descent(full, rows, cols, coher, seen, staged, parts)
    coeff_parts = exchanged(part, bits[1:3], chan_count)
    terms = lax.all_to_all(terms, "pair", 0, 0)
    sent, part = small_call(
        first_update_kernel, total, chan, [sent, terms] + coeff_parts, [blocks, poly]
    )
    full = lax.all_to_all(sent, "pair", 0, 0)
    (terms,) = local_descent(full, rows, cols, coher, seen, staged, [])
    terms = lax.all_to_all(terms, "pair", 0, 0)
    descent, sums = small_call(
        second_sum_kernel,
        total,
        chan,
        [terms, part],
        [block, (chan_count, DIRS, 2 * NP, LANES)],
    )
    sums = lax.all_to_all(sums, "chan", 0, 0)
    return small_call(
        finish_kernel,
        total,
        chan,
        [sent, descent, sums],
        [(8, DIRS, CHANS, BLK), (8, DIRS, CHANS, BLK), (8, DIRS, NP, BLK)],
    )


def solution(mesh):
    placed = (
        P(None, None, "chan", "pair"),
        P("pair", None, None, "chan", None),
        P("pair", None, "chan", None),
        P("pair", None),
        P("pair"),
        P("pair"),
    )
    return jax.shard_map(
        local,
        mesh=mesh,
        in_specs=placed,
        out_specs=(
            P(None, None, "chan", "pair"),
            P(None, None, "chan", "pair"),
            P(None, None, None, "pair"),
        ),
        check_vma=False,
    )
```

```python
import math

import jax
import jax.numpy as jnp
from jax import lax
from jax.experimental import pallas as pl
from jax.experimental.pallas import tpu as pltpu
from jax.sharding import PartitionSpec as P

STATIONS = 256
BLK = 16
NP = 4
RHO = 0.5
MU = 1.0
LANES = 128
CHANS = 8
DIRS = 4
VMEM_LIMIT = 32 * 1024 * 1024
SMALL_LIMIT = 8 * 1024 * 1024


def in_hbm(array):
    return pltpu.with_memory_space_constraint(array, pltpu.HBM)


def lane_iota():
    return lax.broadcasted_iota(jnp.int32, (CHANS, LANES), 1)


def basis_rows(chan, total):
    freq = (chan * CHANS + lax.broadcasted_iota(jnp.int32, (CHANS, LANES), 0)).astype(jnp.float32)
    rows = [jnp.full((CHANS, LANES), math.sqrt(1.0 / total), jnp.float32)]
    for m in range(1, NP):
        rows.append(math.sqrt(2.0 / total) * jnp.cos((math.pi * m) * (freq + 0.5) / total))
    return rows


def project_rows(field, basis):
    return [jnp.sum(basis[m] * field, axis=0, keepdims=True) for m in range(NP)]


def expand_rows(coeffs, basis):
    total = basis[0] * coeffs[0:1]
    for m in range(1, NP):
        total = total + basis[m] * coeffs[m : m + 1]
    return total


def acc_mul(acc, a, b, conj_a=False, conj_b=False, minus=False):
    rr, ii = a[0] * b[0], a[1] * b[1]
    ri, ir = a[0] * b[1], a[1] * b[0]
    sign_ii = -1 if conj_a == conj_b else 1
    sign_ri = -1 if conj_b else 1
    sign_ir = -1 if conj_a else 1
    if minus:
        sign_ii, sign_ri, sign_ir = -sign_ii, -sign_ri, -sign_ir
    sign_rr = -1 if minus else 1

    def put(base, value, sign):
        if base is None:
            return value if sign > 0 else -value
        return base + value if sign > 0 else base - value

    if acc is None:
        real = rr + ii if sign_ii == sign_rr else rr - ii
        if sign_ri == sign_ir:
            imag = ri + ir
        else:
            imag = ri - ir if sign_ri > 0 else ir - ri
        if minus:
            raise ValueError
        return (real, imag)
    return (
        put(put(acc[0], rr, sign_rr), ii, sign_ii),
        put(put(acc[1], ri, sign_ri), ir, sign_ir),
    )


def mat_mul(x, y, acc=None, x_herm=False, y_herm=False, minus=False):
    out = []
    for i in range(2):
        for j in range(2):
            item = None if acc is None else acc[2 * i + j]
            for l in range(2):
                left = x[2 * l + i] if x_herm else x[2 * i + l]
                right = y[2 * j + l] if y_herm else y[2 * l + j]
                item = acc_mul(item, left, right, x_herm, y_herm, minus)
            out.append(item)
    return out


def mat_entry(x, y, i, j, item=None, x_herm=False, y_herm=False):
    for l in range(2):
        left = x[2 * l + i] if x_herm else x[2 * i + l]
        right = y[2 * j + l] if y_herm else y[2 * l + j]
        item = acc_mul(item, left, right, x_herm, y_herm)
    return item


def pairs(list8):
    return [(list8[2 * e], list8[2 * e + 1]) for e in range(4)]


def flat(matrix):
    return [piece for item in matrix for piece in item]


def one_hot(hit):
    return jnp.where(hit, 1.0, 0.0).astype(jnp.bfloat16)


def stage_kernel(rows_ref, cols_ref, marker_ref, *refs):
    part_refs, (keep_ref, spread_ref, sums_ref, total_ref) = refs[:-4], refs[-4:]
    parts = [ref[n] for ref in part_refs for n in range(ref.shape[0])]
    total_ref[...] = sum(parts[1:], parts[0])
    source = lax.broadcasted_iota(jnp.int32, (LANES, LANES), 0)
    target = lax.broadcasted_iota(jnp.int32, (LANES, LANES), 1)
    tables = [target % BLK, target // BLK, target // BLK + 8]
    for n in range(24):
        one = one_hot(source == (n // 3) * BLK + tables[n % 3])
        spread_ref[0:LANES, n * LANES : n * LANES + LANES] = one
        spread_ref[LANES : 2 * LANES, n * LANES : n * LANES + LANES] = one
    for n in range(4):
        sums_ref[0, n * LANES : n * LANES + LANES] = one_hot(target == 2 * n * BLK + source // BLK)
        sums_ref[1, n * LANES : n * LANES + LANES] = one_hot(target == 2 * n * BLK + source % BLK)

    lane = lane_iota()
    for t in range(rows_ref.shape[0]):
        for half in range(2):
            mark = marker_ref[t : t + 1, LANES * half : LANES * half + LANES].astype(jnp.float32)
            keep = jnp.broadcast_to(mark, (CHANS, LANES))
            off_diagonal = rows_ref[t] != cols_ref[t]
            upper = lane // BLK + 8 * half < lane % BLK
            keep = jnp.where((off_diagonal | upper) & (rows_ref[t] >= 0), keep, 0.0)
            keep_ref[t, half] = keep


def stage(marker, rows, cols, parts):
    slots = rows.shape[0]
    vmem = pl.BlockSpec(memory_space=pltpu.VMEM)
    smem = pl.BlockSpec(memory_space=pltpu.SMEM)
    return pl.pallas_call(
        stage_kernel,
        out_shape=[
            pltpu.VMEM((slots, 2, CHANS, LANES), jnp.float32),
            pltpu.VMEM((2 * LANES, 24 * LANES), jnp.bfloat16),
            pltpu.VMEM((2, 4 * LANES, LANES), jnp.bfloat16),
            jax.ShapeDtypeStruct(parts[0].shape[1:], jnp.float32),
        ],
        in_specs=[smem, smem, vmem] + [vmem] * len(parts),
        out_specs=[vmem] * 4,
        compiler_params=pltpu.CompilerParams(vmem_limit_bytes=SMALL_LIMIT),
        cost_estimate=pl.CostEstimate(flops=1_000_000, bytes_accessed=2_000_000, transcendentals=0),
    )(in_hbm(rows), in_hbm(cols), in_hbm(marker), *parts)


def descent_kernel(
    rows_ref,
    cols_ref,
    jones_ref,
    coher_hbm,
    seen_hbm,
    keep_ref,
    spread_ref,
    sums_ref,
    out_ref,
    coher_ref,
    seen_ref,
    wide_ref,
    left_ref,
    res_ref,
    row_ref,
    col_ref,
    coher_sem,
    seen_sem,
):
    slots = rows_ref.shape[0]
    blocks = jones_ref.shape[0]

    def copies(t):
        return (
            pltpu.make_async_copy(coher_hbm.at[t], coher_ref.at[t], coher_sem.at[t]),
            pltpu.make_async_copy(seen_hbm.at[t], seen_ref.at[t], seen_sem.at[t]),
        )

    for t in range(slots):
        for copy in copies(t):
            copy.start()
    out_ref[...] = jnp.zeros_like(out_ref)

    dense = jones_ref[...].reshape(blocks * DIRS * CHANS, LANES)
    high = dense.astype(jnp.bfloat16)
    low = (dense - high.astype(jnp.float32)).astype(jnp.bfloat16)
    split = jnp.concatenate([high, low], axis=1)
    for c in range(12):
        part = slice(256 * c, 256 * c + 256)
        wide = jnp.dot(split, spread_ref[:, part], preferred_element_type=jnp.float32)
        wide_ref[:, :, part] = wide.reshape(blocks * DIRS, CHANS, 256)

    def coher_of(t, k, half):
        kk, odd = k // 2, k % 2
        parts = []
        for e in range(8):
            block = coher_ref[t, e, 16 * kk : 16 * kk + 16, LANES * half : LANES * half + LANES]
            parts.append(block.astype(jnp.float32)[8 * odd : 8 * odd + 8])
        return pairs(parts)

    def expand(block, k, kind):
        return pairs(
            [
                wide_ref[block * DIRS + k, :, (3 * e + kind) * LANES : (3 * e + kind + 1) * LANES]
                for e in range(8)
            ]
        )

    def put(ref, part, item):
        ref[0:8, part * LANES : part * LANES + LANES] = item[0]
        ref[8:16, part * LANES : part * LANES + LANES] = item[1]

    def multiply(t, carry):
        a = jnp.maximum(rows_ref[t], 0)
        b = jnp.maximum(cols_ref[t], 0)
        for copy in copies(t):
            copy.wait()
        for half in range(2):
            acc = []
            for e in range(4):
                both = seen_ref[
                    t, 16 * e : 16 * e + 16, LANES * half : LANES * half + LANES
                ].astype(jnp.float32)
                acc.append((both[0:8], both[8:16]))
            for k in range(DIRS):
                left = mat_mul(expand(a, k, 1 + half), coher_of(t, k, half))
                for e, piece in enumerate(flat(left)):
                    left_ref[half, k, e] = piece
                acc = mat_mul(left, expand(b, k, 0), acc, y_herm=True, minus=True)
            keep = keep_ref[t, half]
            for e, piece in enumerate(flat(acc)):
                res_ref[half, e] = piece * keep
        for k in range(DIRS):
            right = expand(b, k, 0)
            cols = [None] * 4
            for half in range(2):
                res = pairs([res_ref[half, e] for e in range(8)])
                turned = mat_mul(coher_of(t, k, half), right, y_herm=True)
                for e in range(4):
                    item = mat_entry(res, turned, e // 2, e % 2, y_herm=True)
                    put(row_ref.at[t, k, half], e, item)
                left = pairs([left_ref[half, k, e] for e in range(8)])
                for e in range(4):
                    cols[e] = mat_entry(res, left, e // 2, e % 2, cols[e], x_herm=True)
                    if half == 1:
                        put(col_ref.at[t, k], e, cols[e])
        return carry

    lax.fori_loop(0, slots, multiply, 0)

    group = 8

    def total(values, sums):
        high = values.astype(jnp.bfloat16)
        low = (values - high.astype(jnp.float32)).astype(jnp.bfloat16)
        out = jnp.dot(high, sums, preferred_element_type=jnp.float32)
        return out + jnp.dot(low, sums, preferred_element_type=jnp.float32)

    def settle(g, carry):
        t0 = g * group
        rows = total(row_ref[pl.ds(t0, group)].reshape(group * DIRS * 32, 4 * LANES), sums_ref[0])
        cols = total(col_ref[pl.ds(t0, group)].reshape(group * DIRS * 16, 4 * LANES), sums_ref[1])
        rows = rows.reshape(group, DIRS, 2, 2, CHANS, LANES)
        cols = cols.reshape(group, DIRS, 2, CHANS, LANES)
        for n in range(group):
            a = jnp.maximum(rows_ref[t0 + n], 0)
            b = jnp.maximum(cols_ref[t0 + n], 0)
            for k in range(DIRS):
                row = [rows[n, k, 0, c] + pltpu.roll(rows[n, k, 1, c], 8, 1) for c in range(2)]
                row = row[0] + pltpu.roll(row[1], BLK, 1)
                out_ref[a, k] = out_ref[a, k] + row
            for k in range(DIRS):
                col = cols[n, k, 0] + pltpu.roll(cols[n, k, 1], BLK, 1)
                out_ref[b, k] = out_ref[b, k] + col
        return carry

    lax.fori_loop(0, slots // group, settle, 0)


def local_descent(jones_full, rows, cols, coher, seen, staged):
    blocks = jones_full.shape[0]
    slots = rows.shape[0]
    vmem = pl.BlockSpec(memory_space=pltpu.VMEM)
    smem = pl.BlockSpec(memory_space=pltpu.SMEM)
    hbm = pl.BlockSpec(memory_space=pltpu.HBM)
    staged = [pltpu.with_memory_space_constraint(x, pltpu.VMEM) for x in staged]
    return pl.pallas_call(
        descent_kernel,
        out_shape=jax.ShapeDtypeStruct((blocks, DIRS, CHANS, LANES), jnp.float32),
        in_specs=[smem, smem, vmem, hbm, hbm] + [vmem] * 3,
        out_specs=vmem,
        scratch_shapes=[
            pltpu.VMEM(coher.shape, jnp.bfloat16),
            pltpu.VMEM(seen.shape, jnp.bfloat16),
            pltpu.VMEM((blocks * DIRS, CHANS, 24 * LANES), jnp.float32),
            pltpu.VMEM((2, DIRS, 8, CHANS, LANES), jnp.float32),
            pltpu.VMEM((2, 8, CHANS, LANES), jnp.float32),
            pltpu.VMEM((slots, DIRS, 2, 16, 4 * LANES), jnp.float32),
            pltpu.VMEM((slots, DIRS, 16, 4 * LANES), jnp.float32),
            pltpu.SemaphoreType.DMA((slots,)),
            pltpu.SemaphoreType.DMA((slots,)),
        ],
        compiler_params=pltpu.CompilerParams(vmem_limit_bytes=VMEM_LIMIT),
        cost_estimate=pl.CostEstimate(
            flops=40_000_000, bytes_accessed=4_000_000, transcendentals=0
        ),
    )(in_hbm(rows), in_hbm(cols), jones_full, in_hbm(coher), in_hbm(seen), *staged)


def to_dense_kernel(total, chan_ref, start_ref, dense_ref, sent_ref, part_ref):
    basis = basis_rows(chan_ref[0], total)
    for k in range(DIRS):
        field = jnp.concatenate([start_ref[e, k] for e in range(8)], axis=1)
        dense_ref[k] = field
        for n in range(sent_ref.shape[0]):
            sent_ref[n, k] = field
        part_ref[k] = jnp.concatenate(project_rows(field, basis), axis=0)


def descent_sum(terms_ref, k):
    parts = [terms_ref[n, k] for n in range(terms_ref.shape[0])]
    while len(parts) > 1:
        parts = [x + y for x, y in zip(parts[0::2], parts[1::2])]
    return parts[0]


def first_update_kernel(total, chan_ref, jones_ref, terms_ref, *refs):
    coeff_refs, (dense_ref, sent_ref, part_ref) = refs[:-3], refs[-3:]
    basis = basis_rows(chan_ref[0], total)
    for k in range(DIRS):
        coeffs = coeff_refs[0][k]
        for ref in coeff_refs[1:]:
            coeffs = coeffs + ref[k]
        now = jones_ref[k]
        now = now + MU * (
            descent_sum(terms_ref, k) / STATIONS - RHO * (now - expand_rows(coeffs, basis))
        )
        dense_ref[k] = now
        for n in range(sent_ref.shape[0]):
            sent_ref[n, k] = now
        part_ref[k] = jnp.concatenate(project_rows(now, basis), axis=0)


def second_sum_kernel(total, chan_ref, terms_ref, part_ref, descent_ref, sent_ref):
    basis = basis_rows(chan_ref[0], total)
    for k in range(DIRS):
        descent = descent_sum(terms_ref, k)
        descent_ref[k] = descent
        part = jnp.concatenate(
            [part_ref[k], jnp.concatenate(project_rows(descent, basis), axis=0)], axis=0
        )
        for n in range(sent_ref.shape[0]):
            sent_ref[n, k] = part


def finish_kernel(total, chan_ref, jones_ref, descent_ref, sums_ref, sol_ref, du_ref, co_ref):
    basis = basis_rows(chan_ref[0], total)
    for k in range(DIRS):
        both = descent_sum(sums_ref, k)
        coeffs = both[0:NP]
        now = jones_ref[k]
        dual = RHO * (now - expand_rows(coeffs, basis))
        now = now + MU * (descent_ref[k] / STATIONS - dual - dual)
        coeffs = coeffs + (MU / STATIONS) * both[NP : 2 * NP]
        dual = dual + RHO * (now - expand_rows(coeffs, basis))
        for e in range(8):
            part = slice(e * BLK, e * BLK + BLK)
            sol_ref[e, k] = now[:, part]
            du_ref[e, k] = dual[:, part]
            co_ref[e, k] = coeffs[:, part]


def small_call(kernel, total, chan, arrays, shapes):
    vmem = pl.BlockSpec(memory_space=pltpu.VMEM)
    smem = pl.BlockSpec(memory_space=pltpu.SMEM)

    def body(*refs):
        kernel(total, *refs)

    return pl.pallas_call(
        body,
        out_shape=[jax.ShapeDtypeStruct(s, jnp.float32) for s in shapes],
        in_specs=[smem] + [vmem] * len(arrays),
        out_specs=[vmem] * len(shapes),
        compiler_params=pltpu.CompilerParams(vmem_limit_bytes=SMALL_LIMIT),
    )(in_hbm(chan), *arrays)


def flipped(array, bits, count):
    return lax.ppermute(array, "chan", [(i, i ^ bits) for i in range(count)])


def exchanged(part, bits, count):
    masks = [0]
    for bit in bits:
        masks += [m ^ bit for m in masks]
    return [part] + [flipped(part, m, count) for m in masks[1:]]


def local(start, coher, seen, marker, rows, cols):
    pair_count = lax.axis_size("pair")
    chan_count = lax.axis_size("chan")
    total = CHANS * chan_count
    chan = lax.axis_index("chan").astype(jnp.int32).reshape(1)
    coher = coher.reshape(coher.shape[0], 8, DIRS * CHANS, BLK * BLK)
    seen = seen.reshape(seen.shape[0], 8 * CHANS, BLK * BLK)
    block = (DIRS, CHANS, LANES)
    blocks = (pair_count,) + block
    poly = (DIRS, NP, LANES)
    jones, sent, part = small_call(to_dense_kernel, total, chan, [start], [block, blocks, poly])
    full = lax.all_to_all(sent, "pair", 0, 0)
    bits = [1 << i for i in range(chan_count.bit_length() - 1)]
    parts = exchanged(part[None], bits[:1] + bits[3:], chan_count)
    *staged, part = stage(marker, rows, cols, parts)
    terms = local_descent(full, rows, cols, coher, seen, staged)
    coeff_parts = exchanged(part, bits[1:3], chan_count)
    terms = lax.all_to_all(terms, "pair", 0, 0)
    jones, sent, part = small_call(
        first_update_kernel, total, chan, [jones, terms] + coeff_parts, [block, blocks, poly]
    )
    full = lax.all_to_all(sent, "pair", 0, 0)
    terms = local_descent(full, rows, cols, coher, seen, staged)
    terms = lax.all_to_all(terms, "pair", 0, 0)
    descent, sums = small_call(
        second_sum_kernel,
        total,
        chan,
        [terms, part],
        [block, (chan_count, DIRS, 2 * NP, LANES)],
    )
    sums = lax.all_to_all(sums, "chan", 0, 0)
    return small_call(
        finish_kernel,
        total,
        chan,
        [jones, descent, sums],
        [(8, DIRS, CHANS, BLK), (8, DIRS, CHANS, BLK), (8, DIRS, NP, BLK)],
    )


def solution(mesh):
    placed = (
        P(None, None, "chan", "pair"),
        P("pair", None, None, "chan", None),
        P("pair", None, "chan", None),
        P("pair", None),
        P("pair"),
        P("pair"),
    )
    return jax.shard_map(
        local,
        mesh=mesh,
        in_specs=placed,
        out_specs=(
            P(None, None, "chan", "pair"),
            P(None, None, "chan", "pair"),
            P(None, None, None, "pair"),
        ),
        check_vma=False,
    )
```

```python
import math

import jax
import jax.numpy as jnp
from jax import lax
from jax.experimental import pallas as pl
from jax.experimental.pallas import tpu as pltpu
from jax.sharding import PartitionSpec as P

STATIONS = 256
BLK = 16
NP = 4
RHO = 0.5
MU = 1.0
LANES = 128
CHANS = 8
DIRS = 4
VMEM_LIMIT = 32 * 1024 * 1024
SMALL_LIMIT = 8 * 1024 * 1024


def in_hbm(array):
    return pltpu.with_memory_space_constraint(array, pltpu.HBM)


def lane_iota():
    return lax.broadcasted_iota(jnp.int32, (CHANS, LANES), 1)


def basis_rows(chan, total):
    freq = (chan * CHANS + lax.broadcasted_iota(jnp.int32, (CHANS, LANES), 0)).astype(jnp.float32)
    rows = [jnp.full((CHANS, LANES), math.sqrt(1.0 / total), jnp.float32)]
    for m in range(1, NP):
        rows.append(math.sqrt(2.0 / total) * jnp.cos((math.pi * m) * (freq + 0.5) / total))
    return rows


def project_rows(field, basis):
    return [jnp.sum(basis[m] * field, axis=0, keepdims=True) for m in range(NP)]


def expand_rows(coeffs, basis):
    total = basis[0] * coeffs[0:1]
    for m in range(1, NP):
        total = total + basis[m] * coeffs[m : m + 1]
    return total


def acc_mul(acc, a, b, conj_a=False, conj_b=False, minus=False):
    rr, ii = a[0] * b[0], a[1] * b[1]
    ri, ir = a[0] * b[1], a[1] * b[0]
    sign_ii = -1 if conj_a == conj_b else 1
    sign_ri = -1 if conj_b else 1
    sign_ir = -1 if conj_a else 1
    if minus:
        sign_ii, sign_ri, sign_ir = -sign_ii, -sign_ri, -sign_ir
    sign_rr = -1 if minus else 1

    def put(base, value, sign):
        if base is None:
            return value if sign > 0 else -value
        return base + value if sign > 0 else base - value

    if acc is None:
        real = rr + ii if sign_ii == sign_rr else rr - ii
        if sign_ri == sign_ir:
            imag = ri + ir
        else:
            imag = ri - ir if sign_ri > 0 else ir - ri
        if minus:
            raise ValueError
        return (real, imag)
    return (
        put(put(acc[0], rr, sign_rr), ii, sign_ii),
        put(put(acc[1], ri, sign_ri), ir, sign_ir),
    )


def mat_mul(x, y, acc=None, x_herm=False, y_herm=False, minus=False):
    out = []
    for i in range(2):
        for j in range(2):
            item = None if acc is None else acc[2 * i + j]
            for l in range(2):
                left = x[2 * l + i] if x_herm else x[2 * i + l]
                right = y[2 * j + l] if y_herm else y[2 * l + j]
                item = acc_mul(item, left, right, x_herm, y_herm, minus)
            out.append(item)
    return out


def mat_entry(x, y, i, j, item=None, x_herm=False, y_herm=False):
    for l in range(2):
        left = x[2 * l + i] if x_herm else x[2 * i + l]
        right = y[2 * j + l] if y_herm else y[2 * l + j]
        item = acc_mul(item, left, right, x_herm, y_herm)
    return item


def with_sums(matrix):
    return [(item[0], item[1] - item[0], item[0] + item[1]) for item in matrix]


def three(sums, first, second, third):
    terms = (first[0] * first[1], second[0] * second[1], third[0] * third[1])
    return terms if sums is None else tuple(x + y for x, y in zip(sums, terms))


def conj_right(x, y, left, right, sums=None):
    for l, r in zip(left, right):
        re, im = x[l]
        sums = three(sums, (y[r][0], re + im), (im, y[r][1]), (re, y[r][2]))
    return sums


def conj_right_value(sums):
    return (sums[0] + sums[1], sums[0] - sums[2])


def conj_left(x, y, left, right):
    sums = None
    for l, r in zip(left, right):
        re, im = x[l]
        sums = three(sums, (y[r][0], re - im), (im, y[r][2]), (re, y[r][1]))
    return (sums[0] + sums[1], sums[0] + sums[2])


def pairs(list8):
    return [(list8[2 * e], list8[2 * e + 1]) for e in range(4)]


def flat(matrix):
    return [piece for item in matrix for piece in item]


def one_hot(hit):
    return jnp.where(hit, 1.0, 0.0).astype(jnp.bfloat16)


def stage_kernel(rows_ref, cols_ref, marker_ref, *refs):
    part_refs, (keep_ref, spread_ref, sums_ref, total_ref) = refs[:-4], refs[-4:]
    parts = [ref[n] for ref in part_refs for n in range(ref.shape[0])]
    total_ref[...] = sum(parts[1:], parts[0])
    source = lax.broadcasted_iota(jnp.int32, (LANES, LANES), 0)
    target = lax.broadcasted_iota(jnp.int32, (LANES, LANES), 1)
    tables = [target % BLK, target // BLK, target // BLK + 8]
    for n in range(24):
        one = one_hot(source == (n // 3) * BLK + tables[n % 3])
        spread_ref[0:LANES, n * LANES : n * LANES + LANES] = one
        spread_ref[LANES : 2 * LANES, n * LANES : n * LANES + LANES] = one
    column = source // 64 * BLK + source % BLK
    for n in range(4):
        sums_ref[0, n * LANES : n * LANES + LANES] = one_hot(target == 2 * n * BLK + source // BLK)
        sums_ref[1, n * LANES : n * LANES + LANES] = one_hot(target == 2 * n * BLK + column)

    lane = lane_iota()
    for t in range(rows_ref.shape[0]):
        for half in range(2):
            mark = marker_ref[t : t + 1, LANES * half : LANES * half + LANES].astype(jnp.float32)
            keep = jnp.broadcast_to(mark, (CHANS, LANES))
            off_diagonal = rows_ref[t] != cols_ref[t]
            upper = lane // BLK + 8 * half < lane % BLK
            keep = jnp.where((off_diagonal | upper) & (rows_ref[t] >= 0), keep, 0.0)
            keep_ref[t, half] = keep


def stage(marker, rows, cols, parts):
    slots = rows.shape[0]
    vmem = pl.BlockSpec(memory_space=pltpu.VMEM)
    smem = pl.BlockSpec(memory_space=pltpu.SMEM)
    return pl.pallas_call(
        stage_kernel,
        out_shape=[
            pltpu.VMEM((slots, 2, CHANS, LANES), jnp.float32),
            pltpu.VMEM((2 * LANES, 24 * LANES), jnp.bfloat16),
            pltpu.VMEM((2, 4 * LANES, LANES), jnp.bfloat16),
            jax.ShapeDtypeStruct(parts[0].shape[1:], jnp.float32),
        ],
        in_specs=[smem, smem, vmem] + [vmem] * len(parts),
        out_specs=[vmem] * 4,
        compiler_params=pltpu.CompilerParams(vmem_limit_bytes=SMALL_LIMIT),
        cost_estimate=pl.CostEstimate(flops=1_000_000, bytes_accessed=2_000_000, transcendentals=0),
    )(in_hbm(rows), in_hbm(cols), in_hbm(marker), *parts)


def descent_kernel(
    rows_ref,
    cols_ref,
    jones_ref,
    coher_hbm,
    seen_hbm,
    keep_ref,
    spread_ref,
    sums_ref,
    out_ref,
    coher_ref,
    seen_ref,
    wide_ref,
    left_ref,
    res_ref,
    row_ref,
    col_ref,
    coher_sem,
    seen_sem,
):
    slots = rows_ref.shape[0]
    blocks = jones_ref.shape[0]

    def copies(t):
        return (
            pltpu.make_async_copy(coher_hbm.at[t], coher_ref.at[t], coher_sem.at[t]),
            pltpu.make_async_copy(seen_hbm.at[t], seen_ref.at[t], seen_sem.at[t]),
        )

    for t in range(slots):
        for copy in copies(t):
            copy.start()
    out_ref[...] = jnp.zeros_like(out_ref)

    dense = jones_ref[...].reshape(blocks * DIRS * CHANS, LANES)
    high = dense.astype(jnp.bfloat16)
    low = (dense - high.astype(jnp.float32)).astype(jnp.bfloat16)
    split = jnp.concatenate([high, low], axis=1)
    for c in range(12):
        part = slice(256 * c, 256 * c + 256)
        wide = jnp.dot(split, spread_ref[:, part], preferred_element_type=jnp.float32)
        wide_ref[:, :, part] = wide.reshape(blocks * DIRS, CHANS, 256)

    def coher_of(t, k, half):
        kk, odd = k // 2, k % 2
        parts = []
        for e in range(8):
            block = coher_ref[t, e, 16 * kk : 16 * kk + 16, LANES * half : LANES * half + LANES]
            parts.append(block.astype(jnp.float32)[8 * odd : 8 * odd + 8])
        return pairs(parts)

    def expand(block, k, kind):
        return pairs(
            [
                wide_ref[block * DIRS + k, :, (3 * e + kind) * LANES : (3 * e + kind + 1) * LANES]
                for e in range(8)
            ]
        )

    lane = lane_iota()

    def merged(item, dist):
        low = (lane & dist) == 0
        kept = jnp.where(low, item[0], item[1])
        sent = jnp.where(low, item[1], item[0])
        if dist == LANES // 2:
            return kept + pltpu.roll(sent, dist, 1)
        return kept + jnp.take_along_axis(sent, lane ^ dist, axis=1, mode="promise_in_bounds")

    def put(ref, part, item):
        ref[0:8, part * LANES : part * LANES + LANES] = item[0]
        ref[8:16, part * LANES : part * LANES + LANES] = item[1]

    def multiply(t, carry):
        a = jnp.maximum(rows_ref[t], 0)
        b = jnp.maximum(cols_ref[t], 0)
        for copy in copies(t):
            copy.wait()
        for half in range(2):
            acc = []
            for e in range(4):
                both = seen_ref[
                    t, 16 * e : 16 * e + 16, LANES * half : LANES * half + LANES
                ].astype(jnp.float32)
                acc.append((both[0:8], both[8:16]))
            for k in range(DIRS):
                left = mat_mul(expand(a, k, 1 + half), coher_of(t, k, half))
                for e, piece in enumerate(flat(left)):
                    left_ref[half, k, e] = piece
                acc = mat_mul(left, expand(b, k, 0), acc, y_herm=True, minus=True)
            keep = keep_ref[t, half]
            acc = with_sums([(item[0] * keep, item[1] * keep) for item in acc])
            for e, piece in enumerate(flat(acc)):
                res_ref[half, e] = piece
        for k in range(DIRS):
            right = with_sums(expand(b, k, 0))
            cols = [None] * 4
            for half in range(2):
                res = [tuple(res_ref[half, 3 * e + n] for n in range(3)) for e in range(4)]
                coher = coher_of(t, k, half)
                turned = []
                for i in range(2):
                    for j in range(2):
                        sums = conj_right(coher, right, (2 * i, 2 * i + 1), (2 * j, 2 * j + 1))
                        turned.append(conj_right_value(sums))
                for e in range(4):
                    i, j = e // 2, e % 2
                    item = conj_left(turned, res, (2 * j, 2 * j + 1), (2 * i, 2 * i + 1))
                    put(row_ref.at[t, k, half], e, item)
                left = pairs([left_ref[half, k, e] for e in range(8)])
                for e in range(4):
                    i, j = e // 2, e % 2
                    cols[e] = conj_right(left, res, (j, 2 + j), (i, 2 + i), cols[e])
                    if half == 1:
                        col_ref[t, k, :, e * LANES : e * LANES + LANES] = merged(conj_right_value(cols[e]), 64)
        return carry

    lax.fori_loop(0, slots, multiply, 0)

    group = slots

    def total(values, sums):
        high = values.astype(jnp.bfloat16)
        low = values - high.astype(jnp.float32)
        out = jnp.dot(high, sums, preferred_element_type=jnp.float32)
        return out + jnp.dot(low, sums.astype(jnp.float32), preferred_element_type=jnp.float32)

    def settle(g, carry):
        t0 = g * group
        rows = total(row_ref[pl.ds(t0, group)].reshape(group * DIRS * 32, 4 * LANES), sums_ref[0])
        cols = total(col_ref[pl.ds(t0, group)].reshape(group * DIRS * 8, 4 * LANES), sums_ref[1])
        rows = rows.reshape(group, DIRS, 2, 2, CHANS, LANES)
        cols = cols.reshape(group, DIRS, CHANS, LANES)
        for n in range(group):
            a = jnp.maximum(rows_ref[t0 + n], 0)
            b = jnp.maximum(cols_ref[t0 + n], 0)
            for k in range(DIRS):
                row = [rows[n, k, 0, c] + pltpu.roll(rows[n, k, 1, c], 8, 1) for c in range(2)]
                row = row[0] + pltpu.roll(row[1], BLK, 1)
                out_ref[a, k] = out_ref[a, k] + row
            for k in range(DIRS):
                out_ref[b, k] = out_ref[b, k] + cols[n, k]
        return carry

    lax.fori_loop(0, slots // group, settle, 0)


def local_descent(jones_full, rows, cols, coher, seen, staged):
    blocks = jones_full.shape[0]
    slots = rows.shape[0]
    vmem = pl.BlockSpec(memory_space=pltpu.VMEM)
    smem = pl.BlockSpec(memory_space=pltpu.SMEM)
    hbm = pl.BlockSpec(memory_space=pltpu.HBM)
    staged = [pltpu.with_memory_space_constraint(x, pltpu.VMEM) for x in staged]
    return pl.pallas_call(
        descent_kernel,
        out_shape=jax.ShapeDtypeStruct((blocks, DIRS, CHANS, LANES), jnp.float32),
        in_specs=[smem, smem, vmem, hbm, hbm] + [vmem] * 3,
        out_specs=vmem,
        scratch_shapes=[
            pltpu.VMEM(coher.shape, jnp.bfloat16),
            pltpu.VMEM(seen.shape, jnp.bfloat16),
            pltpu.VMEM((blocks * DIRS, CHANS, 24 * LANES), jnp.float32),
            pltpu.VMEM((2, DIRS, 8, CHANS, LANES), jnp.float32),
            pltpu.VMEM((2, 12, CHANS, LANES), jnp.float32),
            pltpu.VMEM((slots, DIRS, 2, 16, 4 * LANES), jnp.float32),
            pltpu.VMEM((slots, DIRS, CHANS, 4 * LANES), jnp.float32),
            pltpu.SemaphoreType.DMA((slots,)),
            pltpu.SemaphoreType.DMA((slots,)),
        ],
        compiler_params=pltpu.CompilerParams(vmem_limit_bytes=VMEM_LIMIT),
        cost_estimate=pl.CostEstimate(
            flops=40_000_000, bytes_accessed=4_000_000, transcendentals=0
        ),
    )(in_hbm(rows), in_hbm(cols), jones_full, in_hbm(coher), in_hbm(seen), *staged)


def to_dense_kernel(total, chan_ref, start_ref, dense_ref, sent_ref, part_ref):
    basis = basis_rows(chan_ref[0], total)
    for k in range(DIRS):
        field = jnp.concatenate([start_ref[e, k] for e in range(8)], axis=1)
        dense_ref[k] = field
        for n in range(sent_ref.shape[0]):
            sent_ref[n, k] = field
        part_ref[k] = jnp.concatenate(project_rows(field, basis), axis=0)


def descent_sum(terms_ref, k):
    parts = [terms_ref[n, k] for n in range(terms_ref.shape[0])]
    while len(parts) > 1:
        parts = [x + y for x, y in zip(parts[0::2], parts[1::2])]
    return parts[0]


def first_update_kernel(total, chan_ref, jones_ref, terms_ref, *refs):
    coeff_refs, (dense_ref, sent_ref, part_ref) = refs[:-3], refs[-3:]
    basis = basis_rows(chan_ref[0], total)
    for k in range(DIRS):
        coeffs = coeff_refs[0][k]
        for ref in coeff_refs[1:]:
            coeffs = coeffs + ref[k]
        now = jones_ref[k]
        now = now + MU * (
            descent_sum(terms_ref, k) / STATIONS - RHO * (now - expand_rows(coeffs, basis))
        )
        dense_ref[k] = now
        for n in range(sent_ref.shape[0]):
            sent_ref[n, k] = now
        part_ref[k] = jnp.concatenate(project_rows(now, basis), axis=0)


def second_sum_kernel(total, chan_ref, terms_ref, part_ref, descent_ref, sent_ref):
    basis = basis_rows(chan_ref[0], total)
    for k in range(DIRS):
        descent = descent_sum(terms_ref, k)
        descent_ref[k] = descent
        part = jnp.concatenate(
            [part_ref[k], jnp.concatenate(project_rows(descent, basis), axis=0)], axis=0
        )
        for n in range(sent_ref.shape[0]):
            sent_ref[n, k] = part


def finish_kernel(total, chan_ref, jones_ref, descent_ref, sums_ref, sol_ref, du_ref, co_ref):
    basis = basis_rows(chan_ref[0], total)
    for k in range(DIRS):
        both = descent_sum(sums_ref, k)
        coeffs = both[0:NP]
        now = jones_ref[k]
        dual = RHO * (now - expand_rows(coeffs, basis))
        now = now + MU * (descent_ref[k] / STATIONS - dual - dual)
        coeffs = coeffs + (MU / STATIONS) * both[NP : 2 * NP]
        dual = dual + RHO * (now - expand_rows(coeffs, basis))
        for e in range(8):
            part = slice(e * BLK, e * BLK + BLK)
            sol_ref[e, k] = now[:, part]
            du_ref[e, k] = dual[:, part]
            co_ref[e, k] = coeffs[:, part]


def small_call(kernel, total, chan, arrays, shapes):
    vmem = pl.BlockSpec(memory_space=pltpu.VMEM)
    smem = pl.BlockSpec(memory_space=pltpu.SMEM)

    def body(*refs):
        kernel(total, *refs)

    return pl.pallas_call(
        body,
        out_shape=[jax.ShapeDtypeStruct(s, jnp.float32) for s in shapes],
        in_specs=[smem] + [vmem] * len(arrays),
        out_specs=[vmem] * len(shapes),
        compiler_params=pltpu.CompilerParams(vmem_limit_bytes=SMALL_LIMIT),
    )(in_hbm(chan), *arrays)


def flipped(array, bits, count):
    return lax.ppermute(array, "chan", [(i, i ^ bits) for i in range(count)])


def exchanged(part, bits, count):
    masks = [0]
    for bit in bits:
        masks += [m ^ bit for m in masks]
    return [part] + [flipped(part, m, count) for m in masks[1:]]


def local(start, coher, seen, marker, rows, cols):
    pair_count = lax.axis_size("pair")
    chan_count = lax.axis_size("chan")
    total = CHANS * chan_count
    chan = lax.axis_index("chan").astype(jnp.int32).reshape(1)
    coher = coher.reshape(coher.shape[0], 8, DIRS * CHANS, BLK * BLK)
    seen = seen.reshape(seen.shape[0], 8 * CHANS, BLK * BLK)
    block = (DIRS, CHANS, LANES)
    blocks = (pair_count,) + block
    poly = (DIRS, NP, LANES)
    jones, sent, part = small_call(to_dense_kernel, total, chan, [start], [block, blocks, poly])
    full = lax.all_to_all(sent, "pair", 0, 0)
    bits = [1 << i for i in range(chan_count.bit_length() - 1)]
    parts = exchanged(part[None], bits[:1] + bits[3:], chan_count)
    *staged, part = stage(marker, rows, cols, parts)
    terms = local_descent(full, rows, cols, coher, seen, staged)
    coeff_parts = exchanged(part, bits[1:3], chan_count)
    terms = lax.all_to_all(terms, "pair", 0, 0)
    jones, sent, part = small_call(
        first_update_kernel, total, chan, [jones, terms] + coeff_parts, [block, blocks, poly]
    )
    full = lax.all_to_all(sent, "pair", 0, 0)
    terms = local_descent(full, rows, cols, coher, seen, staged)
    terms = lax.all_to_all(terms, "pair", 0, 0)
    descent, sums = small_call(
        second_sum_kernel,
        total,
        chan,
        [terms, part],
        [block, (chan_count, DIRS, 2 * NP, LANES)],
    )
    sums = lax.all_to_all(sums, "chan", 0, 0)
    return small_call(
        finish_kernel,
        total,
        chan,
        [jones, descent, sums],
        [(8, DIRS, CHANS, BLK), (8, DIRS, CHANS, BLK), (8, DIRS, NP, BLK)],
    )


def solution(mesh):
    placed = (
        P(None, None, "chan", "pair"),
        P("pair", None, None, "chan", None),
        P("pair", None, "chan", None),
        P("pair", None),
        P("pair"),
        P("pair"),
    )
    return jax.shard_map(
        local,
        mesh=mesh,
        in_specs=placed,
        out_specs=(
            P(None, None, "chan", "pair"),
            P(None, None, "chan", "pair"),
            P(None, None, None, "pair"),
        ),
        check_vma=False,
    )
```

```python
import math

import jax
import jax.numpy as jnp
from jax import lax
from jax.experimental import pallas as pl
from jax.experimental.pallas import tpu as pltpu
from jax.sharding import PartitionSpec as P

STATIONS = 256
BLK = 16
NP = 4
RHO = 0.5
MU = 1.0
LANES = 128
CHANS = 8
DIRS = 4
VMEM_LIMIT = 32 * 1024 * 1024
SMALL_LIMIT = 8 * 1024 * 1024


def in_hbm(array):
    return pltpu.with_memory_space_constraint(array, pltpu.HBM)


def lane_iota():
    return lax.broadcasted_iota(jnp.int32, (CHANS, LANES), 1)


def basis_rows(chan, total):
    freq = (chan * CHANS + lax.broadcasted_iota(jnp.int32, (CHANS, LANES), 0)).astype(jnp.float32)
    rows = [jnp.full((CHANS, LANES), math.sqrt(1.0 / total), jnp.float32)]
    for m in range(1, NP):
        rows.append(math.sqrt(2.0 / total) * jnp.cos((math.pi * m) * (freq + 0.5) / total))
    return rows


def project_rows(field, basis):
    return [jnp.sum(basis[m] * field, axis=0, keepdims=True) for m in range(NP)]


def expand_rows(coeffs, basis):
    total = basis[0] * coeffs[0:1]
    for m in range(1, NP):
        total = total + basis[m] * coeffs[m : m + 1]
    return total


def acc_mul(acc, a, b, conj_a=False, conj_b=False, minus=False):
    rr, ii = a[0] * b[0], a[1] * b[1]
    ri, ir = a[0] * b[1], a[1] * b[0]
    sign_ii = -1 if conj_a == conj_b else 1
    sign_ri = -1 if conj_b else 1
    sign_ir = -1 if conj_a else 1
    if minus:
        sign_ii, sign_ri, sign_ir = -sign_ii, -sign_ri, -sign_ir
    sign_rr = -1 if minus else 1

    def put(base, value, sign):
        if base is None:
            return value if sign > 0 else -value
        return base + value if sign > 0 else base - value

    if acc is None:
        real = rr + ii if sign_ii == sign_rr else rr - ii
        if sign_ri == sign_ir:
            imag = ri + ir
        else:
            imag = ri - ir if sign_ri > 0 else ir - ri
        if minus:
            raise ValueError
        return (real, imag)
    return (
        put(put(acc[0], rr, sign_rr), ii, sign_ii),
        put(put(acc[1], ri, sign_ri), ir, sign_ir),
    )


def mat_mul(x, y, acc=None, x_herm=False, y_herm=False, minus=False):
    out = []
    for i in range(2):
        for j in range(2):
            item = None if acc is None else acc[2 * i + j]
            for l in range(2):
                left = x[2 * l + i] if x_herm else x[2 * i + l]
                right = y[2 * j + l] if y_herm else y[2 * l + j]
                item = acc_mul(item, left, right, x_herm, y_herm, minus)
            out.append(item)
    return out


def mat_entry(x, y, i, j, item=None, x_herm=False, y_herm=False):
    for l in range(2):
        left = x[2 * l + i] if x_herm else x[2 * i + l]
        right = y[2 * j + l] if y_herm else y[2 * l + j]
        item = acc_mul(item, left, right, x_herm, y_herm)
    return item


def with_sums(matrix):
    return [(item[0], item[1] - item[0], item[0] + item[1]) for item in matrix]


def three(sums, first, second, third):
    terms = (first[0] * first[1], second[0] * second[1], third[0] * third[1])
    return terms if sums is None else tuple(x + y for x, y in zip(sums, terms))


def conj_right(x, y, left, right, sums=None):
    for l, r in zip(left, right):
        re, im = x[l]
        sums = three(sums, (y[r][0], re + im), (im, y[r][1]), (re, y[r][2]))
    return sums


def conj_right_value(sums):
    return (sums[0] + sums[1], sums[0] - sums[2])


def conj_left(x, y, left, right):
    sums = None
    for l, r in zip(left, right):
        re, im = x[l]
        sums = three(sums, (y[r][0], re - im), (im, y[r][2]), (re, y[r][1]))
    return (sums[0] + sums[1], sums[0] + sums[2])


def pairs(list8):
    return [(list8[2 * e], list8[2 * e + 1]) for e in range(4)]


def flat(matrix):
    return [piece for item in matrix for piece in item]


def one_hot(hit):
    return jnp.where(hit, 1.0, 0.0).astype(jnp.bfloat16)


def stage_kernel(
    rows_ref, cols_ref, marker_ref, keep_ref, spread_ref, sums_ref, rows_out, cols_out
):
    for t in range(rows_ref.shape[0]):
        rows_out[t] = rows_ref[t]
        cols_out[t] = cols_ref[t]
    source = lax.broadcasted_iota(jnp.int32, (LANES, LANES), 0)
    target = lax.broadcasted_iota(jnp.int32, (LANES, LANES), 1)
    tables = [target % BLK, target // BLK, target // BLK + 8]
    for n in range(24):
        one = one_hot(source == (n // 3) * BLK + tables[n % 3])
        spread_ref[0:LANES, n * LANES : n * LANES + LANES] = one
        spread_ref[LANES : 2 * LANES, n * LANES : n * LANES + LANES] = one
    column = source // 64 * BLK + source % BLK
    for n in range(4):
        sums_ref[0, n * LANES : n * LANES + LANES] = one_hot(target == 2 * n * BLK + source // BLK)
        sums_ref[1, n * LANES : n * LANES + LANES] = one_hot(target == 2 * n * BLK + column)

    lane = lane_iota()
    for t in range(rows_ref.shape[0]):
        for half in range(2):
            mark = marker_ref[t : t + 1, LANES * half : LANES * half + LANES].astype(jnp.float32)
            keep = jnp.broadcast_to(mark, (CHANS, LANES))
            off_diagonal = rows_ref[t] != cols_ref[t]
            upper = lane // BLK + 8 * half < lane % BLK
            keep = jnp.where((off_diagonal | upper) & (rows_ref[t] >= 0), keep, 0.0)
            keep_ref[t, half] = keep


def stage(marker, rows, cols):
    slots = rows.shape[0]
    vmem = pl.BlockSpec(memory_space=pltpu.VMEM)
    smem = pl.BlockSpec(memory_space=pltpu.SMEM)
    return pl.pallas_call(
        stage_kernel,
        out_shape=[
            pltpu.VMEM((slots, 2, CHANS, LANES), jnp.float32),
            pltpu.VMEM((2 * LANES, 24 * LANES), jnp.bfloat16),
            pltpu.VMEM((2, 4 * LANES, LANES), jnp.bfloat16),
            pltpu.SMEM((slots,), jnp.int32),
            pltpu.SMEM((slots,), jnp.int32),
        ],
        in_specs=[smem, smem, vmem],
        out_specs=[vmem] * 3 + [smem] * 2,
        compiler_params=pltpu.CompilerParams(vmem_limit_bytes=SMALL_LIMIT),
        cost_estimate=pl.CostEstimate(flops=1_000_000, bytes_accessed=2_000_000, transcendentals=0),
    )(in_hbm(rows), in_hbm(cols), in_hbm(marker))


def descent_kernel(
    rows_ref,
    cols_ref,
    jones_ref,
    coher_hbm,
    seen_hbm,
    keep_ref,
    spread_ref,
    sums_ref,
    out_ref,
    coher_ref,
    seen_ref,
    wide_ref,
    left_ref,
    res_ref,
    row_ref,
    col_ref,
    coher_sem,
    seen_sem,
):
    slots = rows_ref.shape[0]
    blocks = jones_ref.shape[0]

    def copies(t):
        return (
            pltpu.make_async_copy(coher_hbm.at[t], coher_ref.at[t], coher_sem.at[t]),
            pltpu.make_async_copy(seen_hbm.at[t], seen_ref.at[t], seen_sem.at[t]),
        )

    for t in range(slots):
        for copy in copies(t):
            copy.start()
    out_ref[...] = jnp.zeros_like(out_ref)

    dense = jones_ref[...].reshape(blocks * DIRS * CHANS, LANES)
    high = dense.astype(jnp.bfloat16)
    low = (dense - high.astype(jnp.float32)).astype(jnp.bfloat16)
    split = jnp.concatenate([high, low], axis=1)
    for c in range(12):
        part = slice(256 * c, 256 * c + 256)
        wide = jnp.dot(split, spread_ref[:, part], preferred_element_type=jnp.float32)
        wide_ref[:, :, part] = wide.reshape(blocks * DIRS, CHANS, 256)

    def coher_of(t, k, half):
        kk, odd = k // 2, k % 2
        parts = []
        for e in range(8):
            block = coher_ref[t, e, 16 * kk : 16 * kk + 16, LANES * half : LANES * half + LANES]
            parts.append(block.astype(jnp.float32)[8 * odd : 8 * odd + 8])
        return pairs(parts)

    def expand(block, k, kind):
        return pairs(
            [
                wide_ref[block * DIRS + k, :, (3 * e + kind) * LANES : (3 * e + kind + 1) * LANES]
                for e in range(8)
            ]
        )

    lane = lane_iota()

    def merged(item, dist):
        low = (lane & dist) == 0
        kept = jnp.where(low, item[0], item[1])
        sent = jnp.where(low, item[1], item[0])
        if dist == LANES // 2:
            return kept + pltpu.roll(sent, dist, 1)
        return kept + jnp.take_along_axis(sent, lane ^ dist, axis=1, mode="promise_in_bounds")

    def put(ref, part, item):
        ref[0:8, part * LANES : part * LANES + LANES] = item[0]
        ref[8:16, part * LANES : part * LANES + LANES] = item[1]

    def multiply(t, carry):
        a = jnp.maximum(rows_ref[t], 0)
        b = jnp.maximum(cols_ref[t], 0)
        for copy in copies(t):
            copy.wait()
        for half in range(2):
            acc = []
            for e in range(4):
                both = seen_ref[
                    t, 16 * e : 16 * e + 16, LANES * half : LANES * half + LANES
                ].astype(jnp.float32)
                acc.append((both[0:8], both[8:16]))
            for k in range(DIRS):
                left = mat_mul(expand(a, k, 1 + half), coher_of(t, k, half))
                for e, piece in enumerate(flat(left)):
                    left_ref[half, k, e] = piece
                acc = mat_mul(left, expand(b, k, 0), acc, y_herm=True, minus=True)
            keep = keep_ref[t, half]
            acc = with_sums([(item[0] * keep, item[1] * keep) for item in acc])
            for e, piece in enumerate(flat(acc)):
                res_ref[half, e] = piece
        for k in range(DIRS):
            right = with_sums(expand(b, k, 0))
            cols = [None] * 4
            for half in range(2):
                res = [tuple(res_ref[half, 3 * e + n] for n in range(3)) for e in range(4)]
                coher = coher_of(t, k, half)
                turned = []
                for i in range(2):
                    for j in range(2):
                        sums = conj_right(coher, right, (2 * i, 2 * i + 1), (2 * j, 2 * j + 1))
                        turned.append(conj_right_value(sums))
                for e in range(4):
                    i, j = e // 2, e % 2
                    item = conj_left(turned, res, (2 * j, 2 * j + 1), (2 * i, 2 * i + 1))
                    put(row_ref.at[t, k, half], e, item)
                left = pairs([left_ref[half, k, e] for e in range(8)])
                for e in range(4):
                    i, j = e // 2, e % 2
                    cols[e] = conj_right(left, res, (j, 2 + j), (i, 2 + i), cols[e])
                    if half == 1:
                        col_ref[t, k, :, e * LANES : e * LANES + LANES] = merged(conj_right_value(cols[e]), 64)
        return carry

    lax.fori_loop(0, slots, multiply, 0)

    group = slots

    def total(values, sums):
        high = values.astype(jnp.bfloat16)
        low = values - high.astype(jnp.float32)
        out = jnp.dot(high, sums, preferred_element_type=jnp.float32)
        return out + jnp.dot(low, sums.astype(jnp.float32), preferred_element_type=jnp.float32)

    def settle(g, carry):
        t0 = g * group
        rows = total(row_ref[pl.ds(t0, group)].reshape(group * DIRS * 32, 4 * LANES), sums_ref[0])
        cols = total(col_ref[pl.ds(t0, group)].reshape(group * DIRS * 8, 4 * LANES), sums_ref[1])
        rows = rows.reshape(group, DIRS, 2, 2, CHANS, LANES)
        cols = cols.reshape(group, DIRS, CHANS, LANES)
        for n in range(group):
            a = jnp.maximum(rows_ref[t0 + n], 0)
            b = jnp.maximum(cols_ref[t0 + n], 0)
            for k in range(DIRS):
                row = [rows[n, k, 0, c] + pltpu.roll(rows[n, k, 1, c], 8, 1) for c in range(2)]
                row = row[0] + pltpu.roll(row[1], BLK, 1)
                out_ref[a, k] = out_ref[a, k] + row
            for k in range(DIRS):
                out_ref[b, k] = out_ref[b, k] + cols[n, k]
        return carry

    lax.fori_loop(0, slots // group, settle, 0)


def local_descent(jones_full, rows, cols, coher, seen, staged):
    blocks = jones_full.shape[0]
    slots = rows.shape[0]
    vmem = pl.BlockSpec(memory_space=pltpu.VMEM)
    smem = pl.BlockSpec(memory_space=pltpu.SMEM)
    hbm = pl.BlockSpec(memory_space=pltpu.HBM)
    *staged, rows, cols = staged
    rows = pltpu.with_memory_space_constraint(rows, pltpu.SMEM)
    cols = pltpu.with_memory_space_constraint(cols, pltpu.SMEM)
    staged = [pltpu.with_memory_space_constraint(x, pltpu.VMEM) for x in staged]
    return pl.pallas_call(
        descent_kernel,
        out_shape=jax.ShapeDtypeStruct((blocks, DIRS, CHANS, LANES), jnp.float32),
        in_specs=[smem, smem, vmem, hbm, hbm] + [vmem] * 3,
        out_specs=vmem,
        scratch_shapes=[
            pltpu.VMEM(coher.shape, jnp.bfloat16),
            pltpu.VMEM(seen.shape, jnp.bfloat16),
            pltpu.VMEM((blocks * DIRS, CHANS, 24 * LANES), jnp.float32),
            pltpu.VMEM((2, DIRS, 8, CHANS, LANES), jnp.float32),
            pltpu.VMEM((2, 12, CHANS, LANES), jnp.float32),
            pltpu.VMEM((slots, DIRS, 2, 16, 4 * LANES), jnp.float32),
            pltpu.VMEM((slots, DIRS, CHANS, 4 * LANES), jnp.float32),
            pltpu.SemaphoreType.DMA((slots,)),
            pltpu.SemaphoreType.DMA((slots,)),
        ],
        compiler_params=pltpu.CompilerParams(vmem_limit_bytes=VMEM_LIMIT),
        cost_estimate=pl.CostEstimate(
            flops=40_000_000, bytes_accessed=4_000_000, transcendentals=0
        ),
    )(rows, cols, jones_full, in_hbm(coher), in_hbm(seen), *staged)


def sum_kernel(count, *refs):
    refs[-1][...] = sum([ref[...] for ref in refs[1:count]], refs[0][...])


def sum_of(parts, after=None):
    def body(*refs):
        sum_kernel(len(parts), *refs)

    waited = [] if after is None else [after]
    vmem = pl.BlockSpec(memory_space=pltpu.VMEM)
    return pl.pallas_call(
        body,
        out_shape=jax.ShapeDtypeStruct(parts[0].shape, parts[0].dtype),
        in_specs=[vmem] * len(parts) + [pl.BlockSpec(memory_space=pl.ANY)] * len(waited),
        out_specs=vmem,
        compiler_params=pltpu.CompilerParams(vmem_limit_bytes=SMALL_LIMIT),
    )(*parts, *waited)


def add_kernel(terms_ref, *refs):
    part_refs, (passed_ref, total_ref) = refs[:-2], refs[-2:]
    total_ref[...] = sum([ref[...] for ref in part_refs[1:]], part_refs[0][...])


def add_beside(terms, parts):
    vmem = pl.BlockSpec(memory_space=pltpu.VMEM)
    whole = pl.BlockSpec(memory_space=pl.ANY)
    return pl.pallas_call(
        add_kernel,
        out_shape=[
            jax.ShapeDtypeStruct(terms.shape, terms.dtype),
            jax.ShapeDtypeStruct(parts[0].shape, parts[0].dtype),
        ],
        in_specs=[whole] + [vmem] * len(parts),
        out_specs=[whole, vmem],
        input_output_aliases={0: 0},
        compiler_params=pltpu.CompilerParams(vmem_limit_bytes=SMALL_LIMIT),
    )(terms, *parts)


def to_dense_kernel(total, chan_ref, start_ref, dense_ref, sent_ref, part_ref):
    basis = basis_rows(chan_ref[0], total)
    for k in range(DIRS):
        field = jnp.concatenate([start_ref[e, k] for e in range(8)], axis=1)
        dense_ref[k] = field
        for n in range(sent_ref.shape[0]):
            sent_ref[n, k] = field
        part_ref[k] = jnp.concatenate(project_rows(field, basis), axis=0)


def descent_sum(terms_ref, k):
    parts = [terms_ref[n, k] for n in range(terms_ref.shape[0])]
    while len(parts) > 1:
        parts = [x + y for x, y in zip(parts[0::2], parts[1::2])]
    return parts[0]


def first_update_kernel(total, chan_ref, jones_ref, terms_ref, *refs):
    coeff_refs, (dense_ref, sent_ref, part_ref) = refs[:-3], refs[-3:]
    basis = basis_rows(chan_ref[0], total)
    for k in range(DIRS):
        coeffs = coeff_refs[0][k]
        for ref in coeff_refs[1:]:
            coeffs = coeffs + ref[k]
        now = jones_ref[k]
        now = now + MU * (
            descent_sum(terms_ref, k) / STATIONS - RHO * (now - expand_rows(coeffs, basis))
        )
        dense_ref[k] = now
        for n in range(sent_ref.shape[0]):
            sent_ref[n, k] = now
        part_ref[k] = jnp.concatenate(project_rows(now, basis), axis=0)


def second_sum_kernel(total, chan_ref, terms_ref, part_ref, descent_ref, sent_ref):
    basis = basis_rows(chan_ref[0], total)
    for k in range(DIRS):
        descent = descent_sum(terms_ref, k)
        descent_ref[k] = descent
        part = jnp.concatenate(
            [part_ref[k], jnp.concatenate(project_rows(descent, basis), axis=0)], axis=0
        )
        for n in range(sent_ref.shape[0]):
            sent_ref[n, k] = part


def finish_kernel(total, chan_ref, jones_ref, descent_ref, sums_ref, sol_ref, du_ref, co_ref):
    basis = basis_rows(chan_ref[0], total)
    for k in range(DIRS):
        both = descent_sum(sums_ref, k)
        coeffs = both[0:NP]
        now = jones_ref[k]
        dual = RHO * (now - expand_rows(coeffs, basis))
        now = now + MU * (descent_ref[k] / STATIONS - dual - dual)
        coeffs = coeffs + (MU / STATIONS) * both[NP : 2 * NP]
        dual = dual + RHO * (now - expand_rows(coeffs, basis))
        for e in range(8):
            part = slice(e * BLK, e * BLK + BLK)
            sol_ref[e, k] = now[:, part]
            du_ref[e, k] = dual[:, part]
            co_ref[e, k] = coeffs[:, part]


def small_call(kernel, total, chan, arrays, shapes):
    vmem = pl.BlockSpec(memory_space=pltpu.VMEM)
    smem = pl.BlockSpec(memory_space=pltpu.SMEM)

    def body(*refs):
        kernel(total, *refs)

    return pl.pallas_call(
        body,
        out_shape=[jax.ShapeDtypeStruct(s, jnp.float32) for s in shapes],
        in_specs=[smem] + [vmem] * len(arrays),
        out_specs=[vmem] * len(shapes),
        compiler_params=pltpu.CompilerParams(vmem_limit_bytes=SMALL_LIMIT),
    )(in_hbm(chan), *arrays)


def flipped(array, bits, count):
    return lax.ppermute(array, "chan", [(i, i ^ bits) for i in range(count)])


def exchanged(part, bits, count):
    masks = [0]
    for bit in bits:
        masks += [m ^ bit for m in masks]
    return [part] + [flipped(part, m, count) for m in masks[1:]]


def local(start, coher, seen, marker, rows, cols):
    pair_count = lax.axis_size("pair")
    chan_count = lax.axis_size("chan")
    total = CHANS * chan_count
    chan = lax.axis_index("chan").astype(jnp.int32).reshape(1)
    coher = coher.reshape(coher.shape[0], 8, DIRS * CHANS, BLK * BLK)
    seen = seen.reshape(seen.shape[0], 8 * CHANS, BLK * BLK)
    block = (DIRS, CHANS, LANES)
    blocks = (pair_count,) + block
    poly = (DIRS, NP, LANES)
    jones, sent, part = small_call(to_dense_kernel, total, chan, [in_hbm(start)], [block, blocks, poly])
    full = lax.all_to_all(sent, "pair", 0, 0)
    bits = [1 << i for i in range(chan_count.bit_length() - 1)]
    part = sum_of(exchanged(part, bits[:1], chan_count))
    staged = stage(marker, rows, cols)
    part = sum_of(exchanged(part, bits[1:3], chan_count), after=staged[0])
    terms = local_descent(full, rows, cols, coher, seen, staged)
    terms, coeffs = add_beside(terms, exchanged(part, bits[3:], chan_count))
    terms = lax.all_to_all(terms, "pair", 0, 0)
    jones, sent, part = small_call(
        first_update_kernel, total, chan, [jones, terms, coeffs], [block, blocks, poly]
    )
    full = lax.all_to_all(sent, "pair", 0, 0)
    terms = local_descent(full, rows, cols, coher, seen, staged)
    terms = lax.all_to_all(terms, "pair", 0, 0)
    descent, sums = small_call(
        second_sum_kernel,
        total,
        chan,
        [terms, part],
        [block, (chan_count, DIRS, 2 * NP, LANES)],
    )
    sums = lax.all_to_all(sums, "chan", 0, 0)
    return small_call(
        finish_kernel,
        total,
        chan,
        [jones, descent, sums],
        [(8, DIRS, CHANS, BLK), (8, DIRS, CHANS, BLK), (8, DIRS, NP, BLK)],
    )


def solution(mesh):
    placed = (
        P(None, None, "chan", "pair"),
        P("pair", None, None, "chan", None),
        P("pair", None, "chan", None),
        P("pair", None),
        P("pair"),
        P("pair"),
    )
    return jax.shard_map(
        local,
        mesh=mesh,
        in_specs=placed,
        out_specs=(
            P(None, None, "chan", "pair"),
            P(None, None, "chan", "pair"),
            P(None, None, None, "pair"),
        ),
        check_vma=False,
    )
```

```python
import math

import jax
import jax.numpy as jnp
from jax import lax
from jax.experimental import pallas as pl
from jax.experimental.pallas import tpu as pltpu
from jax.sharding import PartitionSpec as P

STATIONS = 256
BLK = 16
NP = 4
RHO = 0.5
MU = 1.0
LANES = 128
CHANS = 8
DIRS = 4
VMEM_LIMIT = 32 * 1024 * 1024
SMALL_LIMIT = 8 * 1024 * 1024


def in_hbm(array):
    return pltpu.with_memory_space_constraint(array, pltpu.HBM)


def lane_iota():
    return lax.broadcasted_iota(jnp.int32, (CHANS, LANES), 1)


def basis_rows(chan, total):
    freq = (chan * CHANS + lax.broadcasted_iota(jnp.int32, (CHANS, LANES), 0)).astype(jnp.float32)
    rows = [jnp.full((CHANS, LANES), math.sqrt(1.0 / total), jnp.float32)]
    for m in range(1, NP):
        rows.append(math.sqrt(2.0 / total) * jnp.cos((math.pi * m) * (freq + 0.5) / total))
    return rows


def project_rows(field, basis):
    return [jnp.sum(basis[m] * field, axis=0, keepdims=True) for m in range(NP)]


def expand_rows(coeffs, basis):
    total = basis[0] * coeffs[0:1]
    for m in range(1, NP):
        total = total + basis[m] * coeffs[m : m + 1]
    return total


def acc_mul(acc, a, b, conj_a=False, conj_b=False, minus=False):
    rr, ii = a[0] * b[0], a[1] * b[1]
    ri, ir = a[0] * b[1], a[1] * b[0]
    sign_ii = -1 if conj_a == conj_b else 1
    sign_ri = -1 if conj_b else 1
    sign_ir = -1 if conj_a else 1
    if minus:
        sign_ii, sign_ri, sign_ir = -sign_ii, -sign_ri, -sign_ir
    sign_rr = -1 if minus else 1

    def put(base, value, sign):
        if base is None:
            return value if sign > 0 else -value
        return base + value if sign > 0 else base - value

    if acc is None:
        real = rr + ii if sign_ii == sign_rr else rr - ii
        if sign_ri == sign_ir:
            imag = ri + ir
        else:
            imag = ri - ir if sign_ri > 0 else ir - ri
        if minus:
            raise ValueError
        return (real, imag)
    return (
        put(put(acc[0], rr, sign_rr), ii, sign_ii),
        put(put(acc[1], ri, sign_ri), ir, sign_ir),
    )


def mat_mul(x, y, acc=None, x_herm=False, y_herm=False, minus=False):
    out = []
    for i in range(2):
        for j in range(2):
            item = None if acc is None else acc[2 * i + j]
            for l in range(2):
                left = x[2 * l + i] if x_herm else x[2 * i + l]
                right = y[2 * j + l] if y_herm else y[2 * l + j]
                item = acc_mul(item, left, right, x_herm, y_herm, minus)
            out.append(item)
    return out


def mat_entry(x, y, i, j, item=None, x_herm=False, y_herm=False):
    for l in range(2):
        left = x[2 * l + i] if x_herm else x[2 * i + l]
        right = y[2 * j + l] if y_herm else y[2 * l + j]
        item = acc_mul(item, left, right, x_herm, y_herm)
    return item


def with_sums(matrix):
    return [(item[0], item[1] - item[0], item[0] + item[1]) for item in matrix]


def three(sums, first, second, third):
    terms = (first[0] * first[1], second[0] * second[1], third[0] * third[1])
    return terms if sums is None else tuple(x + y for x, y in zip(sums, terms))


def conj_right(x, y, left, right, sums=None):
    for l, r in zip(left, right):
        re, im = x[l]
        sums = three(sums, (y[r][0], re + im), (im, y[r][1]), (re, y[r][2]))
    return sums


def conj_right_value(sums):
    return (sums[0] + sums[1], sums[0] - sums[2])


def conj_left(x, y, left, right):
    sums = None
    for l, r in zip(left, right):
        re, im = x[l]
        sums = three(sums, (y[r][0], re - im), (im, y[r][2]), (re, y[r][1]))
    return (sums[0] + sums[1], sums[0] + sums[2])


def pairs(list8):
    return [(list8[2 * e], list8[2 * e + 1]) for e in range(4)]


def flat(matrix):
    return [piece for item in matrix for piece in item]


def one_hot(hit):
    return jnp.where(hit, 1.0, 0.0).astype(jnp.bfloat16)


def stage_kernel(
    rows_ref, cols_ref, marker_ref, keep_ref, spread_ref, sums_ref, rows_out, cols_out
):
    for t in range(rows_ref.shape[0]):
        rows_out[t] = rows_ref[t]
        cols_out[t] = cols_ref[t]
    source = lax.broadcasted_iota(jnp.int32, (LANES, LANES), 0)
    target = lax.broadcasted_iota(jnp.int32, (LANES, LANES), 1)
    tables = [target % BLK, target // BLK, target // BLK + 8]
    for n in range(24):
        one = one_hot(source == (n // 3) * BLK + tables[n % 3])
        spread_ref[0:LANES, n * LANES : n * LANES + LANES] = one
        spread_ref[LANES : 2 * LANES, n * LANES : n * LANES + LANES] = one
    column = source // 64 * BLK + source % BLK
    for n in range(4):
        sums_ref[0, n * LANES : n * LANES + LANES] = one_hot(target == 2 * n * BLK + source // BLK)
        sums_ref[1, n * LANES : n * LANES + LANES] = one_hot(target == 2 * n * BLK + column)

    lane = lane_iota()
    for t in range(rows_ref.shape[0]):
        for half in range(2):
            mark = marker_ref[t : t + 1, LANES * half : LANES * half + LANES].astype(jnp.float32)
            keep = jnp.broadcast_to(mark, (CHANS, LANES))
            off_diagonal = rows_ref[t] != cols_ref[t]
            upper = lane // BLK + 8 * half < lane % BLK
            keep = jnp.where((off_diagonal | upper) & (rows_ref[t] >= 0), keep, 0.0)
            keep_ref[t, half] = keep


def stage(marker, rows, cols):
    slots = rows.shape[0]
    vmem = pl.BlockSpec(memory_space=pltpu.VMEM)
    smem = pl.BlockSpec(memory_space=pltpu.SMEM)
    return pl.pallas_call(
        stage_kernel,
        out_shape=[
            pltpu.VMEM((slots, 2, CHANS, LANES), jnp.float32),
            pltpu.VMEM((2 * LANES, 24 * LANES), jnp.bfloat16),
            pltpu.VMEM((2, 4 * LANES, LANES), jnp.bfloat16),
            pltpu.SMEM((slots,), jnp.int32),
            pltpu.SMEM((slots,), jnp.int32),
        ],
        in_specs=[smem, smem, vmem],
        out_specs=[vmem] * 3 + [smem] * 2,
        compiler_params=pltpu.CompilerParams(vmem_limit_bytes=SMALL_LIMIT),
        cost_estimate=pl.CostEstimate(flops=1_000_000, bytes_accessed=2_000_000, transcendentals=0),
    )(in_hbm(rows), in_hbm(cols), in_hbm(marker))


def descent_kernel(
    rows_ref,
    cols_ref,
    jones_ref,
    coher_hbm,
    seen_hbm,
    keep_ref,
    spread_ref,
    sums_ref,
    out_ref,
    coher_ref,
    seen_ref,
    wide_ref,
    left_ref,
    res_ref,
    row_ref,
    col_ref,
    coher_sem,
    seen_sem,
):
    slots = rows_ref.shape[0]
    blocks = jones_ref.shape[0]

    def copies(t):
        return (
            pltpu.make_async_copy(coher_hbm.at[t], coher_ref.at[t], coher_sem.at[t]),
            pltpu.make_async_copy(seen_hbm.at[t], seen_ref.at[t], seen_sem.at[t]),
        )

    for t in range(slots):
        for copy in copies(t):
            copy.start()
    out_ref[...] = jnp.zeros_like(out_ref)

    dense = jones_ref[...].reshape(blocks * DIRS * CHANS, LANES)
    high = dense.astype(jnp.bfloat16)
    low = (dense - high.astype(jnp.float32)).astype(jnp.bfloat16)
    split = jnp.concatenate([high, low], axis=1)
    for c in range(12):
        part = slice(256 * c, 256 * c + 256)
        wide = jnp.dot(split, spread_ref[:, part], preferred_element_type=jnp.float32)
        wide_ref[:, :, part] = wide.reshape(blocks * DIRS, CHANS, 256)

    def coher_of(t, k, half):
        kk, odd = k // 2, k % 2
        parts = []
        for e in range(8):
            block = coher_ref[t, e, 16 * kk : 16 * kk + 16, LANES * half : LANES * half + LANES]
            parts.append(block.astype(jnp.float32)[8 * odd : 8 * odd + 8])
        return pairs(parts)

    def expand(block, k, kind):
        return pairs(
            [
                wide_ref[block * DIRS + k, :, (3 * e + kind) * LANES : (3 * e + kind + 1) * LANES]
                for e in range(8)
            ]
        )

    lane = lane_iota()

    def merged(item, dist):
        low = (lane & dist) == 0
        kept = jnp.where(low, item[0], item[1])
        sent = jnp.where(low, item[1], item[0])
        if dist == LANES // 2:
            return kept + pltpu.roll(sent, dist, 1)
        return kept + jnp.take_along_axis(sent, lane ^ dist, axis=1, mode="promise_in_bounds")

    def put(ref, part, item):
        ref[0:8, part * LANES : part * LANES + LANES] = item[0]
        ref[8:16, part * LANES : part * LANES + LANES] = item[1]

    def multiply(t, carry):
        a = jnp.maximum(rows_ref[t], 0)
        b = jnp.maximum(cols_ref[t], 0)
        for copy in copies(t):
            copy.wait()

        @pl.when(rows_ref[t] >= 0)
        def _():
            for half in range(2):
                acc = []
                for e in range(4):
                    both = seen_ref[
                        t, 16 * e : 16 * e + 16, LANES * half : LANES * half + LANES
                    ].astype(jnp.float32)
                    acc.append((both[0:8], both[8:16]))
                for k in range(DIRS):
                    left = mat_mul(expand(a, k, 1 + half), coher_of(t, k, half))
                    for e, piece in enumerate(flat(left)):
                        left_ref[half, k, e] = piece
                    acc = mat_mul(left, expand(b, k, 0), acc, y_herm=True, minus=True)
                keep = keep_ref[t, half]
                acc = with_sums([(item[0] * keep, item[1] * keep) for item in acc])
                for e, piece in enumerate(flat(acc)):
                    res_ref[half, e] = piece
            for k in range(DIRS):
                right = with_sums(expand(b, k, 0))
                cols = [None] * 4
                for half in range(2):
                    res = [tuple(res_ref[half, 3 * e + n] for n in range(3)) for e in range(4)]
                    coher = coher_of(t, k, half)
                    turned = []
                    for i in range(2):
                        for j in range(2):
                            sums = conj_right(coher, right, (2 * i, 2 * i + 1), (2 * j, 2 * j + 1))
                            turned.append(conj_right_value(sums))
                    for e in range(4):
                        i, j = e // 2, e % 2
                        item = conj_left(turned, res, (2 * j, 2 * j + 1), (2 * i, 2 * i + 1))
                        put(row_ref.at[t, k, half], e, item)
                    left = pairs([left_ref[half, k, e] for e in range(8)])
                    for e in range(4):
                        i, j = e // 2, e % 2
                        cols[e] = conj_right(left, res, (j, 2 + j), (i, 2 + i), cols[e])
                        if half == 1:
                            col_ref[t, k, :, e * LANES : e * LANES + LANES] = merged(conj_right_value(cols[e]), 64)

        return carry

    lax.fori_loop(0, slots, multiply, 0)

    group = slots

    def total(values, sums):
        high = values.astype(jnp.bfloat16)
        low = values - high.astype(jnp.float32)
        out = jnp.dot(high, sums, preferred_element_type=jnp.float32)
        return out + jnp.dot(low, sums.astype(jnp.float32), preferred_element_type=jnp.float32)

    def settle(g, carry):
        t0 = g * group
        rows = total(row_ref[pl.ds(t0, group)].reshape(group * DIRS * 32, 4 * LANES), sums_ref[0])
        cols = total(col_ref[pl.ds(t0, group)].reshape(group * DIRS * 8, 4 * LANES), sums_ref[1])
        rows = rows.reshape(group, DIRS, 2, 2, CHANS, LANES)
        cols = cols.reshape(group, DIRS, CHANS, LANES)
        for n in range(group):
            a = jnp.maximum(rows_ref[t0 + n], 0)
            b = jnp.maximum(cols_ref[t0 + n], 0)
            live = rows_ref[t0 + n] >= 0
            for k in range(DIRS):
                row = [rows[n, k, 0, c] + pltpu.roll(rows[n, k, 1, c], 8, 1) for c in range(2)]
                row = row[0] + pltpu.roll(row[1], BLK, 1)
                out_ref[a, k] = out_ref[a, k] + jnp.where(live, row, 0.0)
            for k in range(DIRS):
                out_ref[b, k] = out_ref[b, k] + jnp.where(live, cols[n, k], 0.0)
        return carry

    lax.fori_loop(0, slots // group, settle, 0)


def local_descent(jones_full, rows, cols, coher, seen, staged):
    blocks = jones_full.shape[0]
    slots = rows.shape[0]
    vmem = pl.BlockSpec(memory_space=pltpu.VMEM)
    smem = pl.BlockSpec(memory_space=pltpu.SMEM)
    hbm = pl.BlockSpec(memory_space=pltpu.HBM)
    *staged, rows, cols = staged
    rows = pltpu.with_memory_space_constraint(rows, pltpu.SMEM)
    cols = pltpu.with_memory_space_constraint(cols, pltpu.SMEM)
    staged = [pltpu.with_memory_space_constraint(x, pltpu.VMEM) for x in staged]
    return pl.pallas_call(
        descent_kernel,
        out_shape=jax.ShapeDtypeStruct((blocks, DIRS, CHANS, LANES), jnp.float32),
        in_specs=[smem, smem, vmem, hbm, hbm] + [vmem] * 3,
        out_specs=vmem,
        scratch_shapes=[
            pltpu.VMEM(coher.shape, jnp.bfloat16),
            pltpu.VMEM(seen.shape, jnp.bfloat16),
            pltpu.VMEM((blocks * DIRS, CHANS, 24 * LANES), jnp.float32),
            pltpu.VMEM((2, DIRS, 8, CHANS, LANES), jnp.float32),
            pltpu.VMEM((2, 12, CHANS, LANES), jnp.float32),
            pltpu.VMEM((slots, DIRS, 2, 16, 4 * LANES), jnp.float32),
            pltpu.VMEM((slots, DIRS, CHANS, 4 * LANES), jnp.float32),
            pltpu.SemaphoreType.DMA((slots,)),
            pltpu.SemaphoreType.DMA((slots,)),
        ],
        compiler_params=pltpu.CompilerParams(vmem_limit_bytes=VMEM_LIMIT),
        cost_estimate=pl.CostEstimate(
            flops=40_000_000, bytes_accessed=4_000_000, transcendentals=0
        ),
    )(rows, cols, jones_full, in_hbm(coher), in_hbm(seen), *staged)


def sum_kernel(count, *refs):
    refs[-1][...] = sum([ref[...] for ref in refs[1:count]], refs[0][...])


def sum_of(parts, after=None):
    def body(*refs):
        sum_kernel(len(parts), *refs)

    waited = [] if after is None else [after]
    vmem = pl.BlockSpec(memory_space=pltpu.VMEM)
    return pl.pallas_call(
        body,
        out_shape=jax.ShapeDtypeStruct(parts[0].shape, parts[0].dtype),
        in_specs=[vmem] * len(parts) + [pl.BlockSpec(memory_space=pl.ANY)] * len(waited),
        out_specs=vmem,
        compiler_params=pltpu.CompilerParams(vmem_limit_bytes=SMALL_LIMIT),
    )(*parts, *waited)


def add_kernel(terms_ref, *refs):
    part_refs, (passed_ref, total_ref) = refs[:-2], refs[-2:]
    total_ref[...] = sum([ref[...] for ref in part_refs[1:]], part_refs[0][...])


def add_beside(terms, parts):
    vmem = pl.BlockSpec(memory_space=pltpu.VMEM)
    whole = pl.BlockSpec(memory_space=pl.ANY)
    return pl.pallas_call(
        add_kernel,
        out_shape=[
            jax.ShapeDtypeStruct(terms.shape, terms.dtype),
            jax.ShapeDtypeStruct(parts[0].shape, parts[0].dtype),
        ],
        in_specs=[whole] + [vmem] * len(parts),
        out_specs=[whole, vmem],
        input_output_aliases={0: 0},
        compiler_params=pltpu.CompilerParams(vmem_limit_bytes=SMALL_LIMIT),
    )(terms, *parts)


def to_dense_kernel(total, chan_ref, start_ref, dense_ref, sent_ref, part_ref):
    basis = basis_rows(chan_ref[0], total)
    for k in range(DIRS):
        field = jnp.concatenate([start_ref[e, k] for e in range(8)], axis=1)
        dense_ref[k] = field
        for n in range(sent_ref.shape[0]):
            sent_ref[n, k] = field
        part_ref[k] = jnp.concatenate(project_rows(field, basis), axis=0)


def descent_sum(terms_ref, k):
    parts = [terms_ref[n, k] for n in range(terms_ref.shape[0])]
    while len(parts) > 1:
        parts = [x + y for x, y in zip(parts[0::2], parts[1::2])]
    return parts[0]


def first_update_kernel(total, chan_ref, jones_ref, terms_ref, *refs):
    coeff_refs, (dense_ref, sent_ref, part_ref) = refs[:-3], refs[-3:]
    basis = basis_rows(chan_ref[0], total)
    for k in range(DIRS):
        coeffs = coeff_refs[0][k]
        for ref in coeff_refs[1:]:
            coeffs = coeffs + ref[k]
        now = jones_ref[k]
        now = now + MU * (
            descent_sum(terms_ref, k) / STATIONS - RHO * (now - expand_rows(coeffs, basis))
        )
        dense_ref[k] = now
        for n in range(sent_ref.shape[0]):
            sent_ref[n, k] = now
        part_ref[k] = jnp.concatenate(project_rows(now, basis), axis=0)


def second_sum_kernel(total, chan_ref, terms_ref, part_ref, descent_ref, sent_ref):
    basis = basis_rows(chan_ref[0], total)
    for k in range(DIRS):
        descent = descent_sum(terms_ref, k)
        descent_ref[k] = descent
        part = jnp.concatenate(
            [part_ref[k], jnp.concatenate(project_rows(descent, basis), axis=0)], axis=0
        )
        for n in range(sent_ref.shape[0]):
            sent_ref[n, k] = part


def finish_kernel(total, chan_ref, jones_ref, descent_ref, sums_ref, sol_ref, du_ref, co_ref):
    basis = basis_rows(chan_ref[0], total)
    for k in range(DIRS):
        both = descent_sum(sums_ref, k)
        coeffs = both[0:NP]
        now = jones_ref[k]
        dual = RHO * (now - expand_rows(coeffs, basis))
        now = now + MU * (descent_ref[k] / STATIONS - dual - dual)
        coeffs = coeffs + (MU / STATIONS) * both[NP : 2 * NP]
        dual = dual + RHO * (now - expand_rows(coeffs, basis))
        for e in range(8):
            part = slice(e * BLK, e * BLK + BLK)
            sol_ref[e, k] = now[:, part]
            du_ref[e, k] = dual[:, part]
            co_ref[e, k] = coeffs[:, part]


def small_call(kernel, total, chan, arrays, shapes):
    vmem = pl.BlockSpec(memory_space=pltpu.VMEM)
    smem = pl.BlockSpec(memory_space=pltpu.SMEM)

    def body(*refs):
        kernel(total, *refs)

    return pl.pallas_call(
        body,
        out_shape=[jax.ShapeDtypeStruct(s, jnp.float32) for s in shapes],
        in_specs=[smem] + [vmem] * len(arrays),
        out_specs=[vmem] * len(shapes),
        compiler_params=pltpu.CompilerParams(vmem_limit_bytes=SMALL_LIMIT),
    )(in_hbm(chan), *arrays)


def flipped(array, bits, count):
    return lax.ppermute(array, "chan", [(i, i ^ bits) for i in range(count)])


def exchanged(part, bits, count):
    masks = [0]
    for bit in bits:
        masks += [m ^ bit for m in masks]
    return [part] + [flipped(part, m, count) for m in masks[1:]]


def local(start, coher, seen, marker, rows, cols):
    pair_count = lax.axis_size("pair")
    chan_count = lax.axis_size("chan")
    total = CHANS * chan_count
    chan = lax.axis_index("chan").astype(jnp.int32).reshape(1)
    coher = coher.reshape(coher.shape[0], 8, DIRS * CHANS, BLK * BLK)
    seen = seen.reshape(seen.shape[0], 8 * CHANS, BLK * BLK)
    block = (DIRS, CHANS, LANES)
    blocks = (pair_count,) + block
    poly = (DIRS, NP, LANES)
    jones, sent, part = small_call(to_dense_kernel, total, chan, [in_hbm(start)], [block, blocks, poly])
    full = lax.all_to_all(sent, "pair", 0, 0)
    bits = [1 << i for i in range(chan_count.bit_length() - 1)]
    part = sum_of(exchanged(part, bits[:1], chan_count))
    staged = stage(marker, rows, cols)
    part = sum_of(exchanged(part, bits[1:3], chan_count), after=staged[0])
    terms = local_descent(full, rows, cols, coher, seen, staged)
    terms, coeffs = add_beside(terms, exchanged(part, bits[3:], chan_count))
    terms = lax.all_to_all(terms, "pair", 0, 0)
    jones, sent, part = small_call(
        first_update_kernel, total, chan, [jones, terms, coeffs], [block, blocks, poly]
    )
    full = lax.all_to_all(sent, "pair", 0, 0)
    terms = local_descent(full, rows, cols, coher, seen, staged)
    terms = lax.all_to_all(terms, "pair", 0, 0)
    descent, sums = small_call(
        second_sum_kernel,
        total,
        chan,
        [terms, part],
        [block, (chan_count, DIRS, 2 * NP, LANES)],
    )
    sums = lax.all_to_all(sums, "chan", 0, 0)
    return small_call(
        finish_kernel,
        total,
        chan,
        [jones, descent, sums],
        [(8, DIRS, CHANS, BLK), (8, DIRS, CHANS, BLK), (8, DIRS, NP, BLK)],
    )


def solution(mesh):
    placed = (
        P(None, None, "chan", "pair"),
        P("pair", None, None, "chan", None),
        P("pair", None, "chan", None),
        P("pair", None),
        P("pair"),
        P("pair"),
    )
    return jax.shard_map(
        local,
        mesh=mesh,
        in_specs=placed,
        out_specs=(
            P(None, None, "chan", "pair"),
            P(None, None, "chan", "pair"),
            P(None, None, None, "pair"),
        ),
        check_vma=False,
    )
```

```python
import math

import jax
import jax.numpy as jnp
from jax import lax
from jax.experimental import pallas as pl
from jax.experimental.pallas import tpu as pltpu
from jax.sharding import PartitionSpec as P

STATIONS = 256
BLK = 16
NP = 4
RHO = 0.5
MU = 1.0
LANES = 128
CHANS = 8
DIRS = 4
VMEM_LIMIT = 32 * 1024 * 1024
SMALL_LIMIT = 8 * 1024 * 1024


def in_hbm(array):
    return pltpu.with_memory_space_constraint(array, pltpu.HBM)


def lane_iota():
    return lax.broadcasted_iota(jnp.int32, (CHANS, LANES), 1)


def basis_rows(chan, total):
    freq = (chan * CHANS + lax.broadcasted_iota(jnp.int32, (CHANS, LANES), 0)).astype(jnp.float32)
    rows = [jnp.full((CHANS, LANES), math.sqrt(1.0 / total), jnp.float32)]
    for m in range(1, NP):
        rows.append(math.sqrt(2.0 / total) * jnp.cos((math.pi * m) * (freq + 0.5) / total))
    return rows


def project_rows(field, basis):
    return [jnp.sum(basis[m] * field, axis=0, keepdims=True) for m in range(NP)]


def expand_rows(coeffs, basis):
    total = basis[0] * coeffs[0:1]
    for m in range(1, NP):
        total = total + basis[m] * coeffs[m : m + 1]
    return total


def acc_mul(acc, a, b, conj_a=False, conj_b=False, minus=False):
    rr, ii = a[0] * b[0], a[1] * b[1]
    ri, ir = a[0] * b[1], a[1] * b[0]
    sign_ii = -1 if conj_a == conj_b else 1
    sign_ri = -1 if conj_b else 1
    sign_ir = -1 if conj_a else 1
    if minus:
        sign_ii, sign_ri, sign_ir = -sign_ii, -sign_ri, -sign_ir
    sign_rr = -1 if minus else 1

    def put(base, value, sign):
        if base is None:
            return value if sign > 0 else -value
        return base + value if sign > 0 else base - value

    if acc is None:
        real = rr + ii if sign_ii == sign_rr else rr - ii
        if sign_ri == sign_ir:
            imag = ri + ir
        else:
            imag = ri - ir if sign_ri > 0 else ir - ri
        if minus:
            raise ValueError
        return (real, imag)
    return (
        put(put(acc[0], rr, sign_rr), ii, sign_ii),
        put(put(acc[1], ri, sign_ri), ir, sign_ir),
    )


def mat_mul(x, y, acc=None, x_herm=False, y_herm=False, minus=False):
    out = []
    for i in range(2):
        for j in range(2):
            item = None if acc is None else acc[2 * i + j]
            for l in range(2):
                left = x[2 * l + i] if x_herm else x[2 * i + l]
                right = y[2 * j + l] if y_herm else y[2 * l + j]
                item = acc_mul(item, left, right, x_herm, y_herm, minus)
            out.append(item)
    return out


def mat_entry(x, y, i, j, item=None, x_herm=False, y_herm=False):
    for l in range(2):
        left = x[2 * l + i] if x_herm else x[2 * i + l]
        right = y[2 * j + l] if y_herm else y[2 * l + j]
        item = acc_mul(item, left, right, x_herm, y_herm)
    return item


def with_sums(matrix):
    return [(item[0], item[1] - item[0], item[0] + item[1]) for item in matrix]


def three(sums, first, second, third):
    terms = (first[0] * first[1], second[0] * second[1], third[0] * third[1])
    return terms if sums is None else tuple(x + y for x, y in zip(sums, terms))


def conj_right(x, y, left, right, sums=None):
    for l, r in zip(left, right):
        re, im = x[l]
        sums = three(sums, (y[r][0], re + im), (im, y[r][1]), (re, y[r][2]))
    return sums


def conj_right_value(sums):
    return (sums[0] + sums[1], sums[0] - sums[2])


def conj_left(x, y, left, right):
    sums = None
    for l, r in zip(left, right):
        re, im = x[l]
        sums = three(sums, (y[r][0], re - im), (im, y[r][2]), (re, y[r][1]))
    return (sums[0] + sums[1], sums[0] + sums[2])


def pairs(list8):
    return [(list8[2 * e], list8[2 * e + 1]) for e in range(4)]


def flat(matrix):
    return [piece for item in matrix for piece in item]


def one_hot(hit):
    return jnp.where(hit, 1.0, 0.0).astype(jnp.bfloat16)


def stage_kernel(
    rows_ref, cols_ref, marker_ref, keep_ref, spread_ref, sums_ref, rows_out, cols_out
):
    for t in range(rows_ref.shape[0]):
        rows_out[t] = rows_ref[t]
        cols_out[t] = cols_ref[t]
    source = lax.broadcasted_iota(jnp.int32, (LANES, LANES), 0)
    target = lax.broadcasted_iota(jnp.int32, (LANES, LANES), 1)
    tables = [target % BLK, target // BLK, target // BLK + 8]
    for n in range(24):
        one = one_hot(source == (n // 3) * BLK + tables[n % 3])
        spread_ref[0:LANES, n * LANES : n * LANES + LANES] = one
        spread_ref[LANES : 2 * LANES, n * LANES : n * LANES + LANES] = one
    column = source // 64 * BLK + source % BLK
    for n in range(4):
        sums_ref[0, n * LANES : n * LANES + LANES] = one_hot(target == 2 * n * BLK + source // BLK)
        sums_ref[1, n * LANES : n * LANES + LANES] = one_hot(target == 2 * n * BLK + column)

    lane = lane_iota()
    for t in range(rows_ref.shape[0]):
        for half in range(2):
            mark = marker_ref[t : t + 1, LANES * half : LANES * half + LANES].astype(jnp.float32)
            keep = jnp.broadcast_to(mark, (CHANS, LANES))
            off_diagonal = rows_ref[t] != cols_ref[t]
            upper = lane // BLK + 8 * half < lane % BLK
            keep = jnp.where((off_diagonal | upper) & (rows_ref[t] >= 0), keep, 0.0)
            keep_ref[t, half] = keep


def stage(marker, rows, cols):
    slots = rows.shape[0]
    vmem = pl.BlockSpec(memory_space=pltpu.VMEM)
    smem = pl.BlockSpec(memory_space=pltpu.SMEM)
    return pl.pallas_call(
        stage_kernel,
        out_shape=[
            pltpu.VMEM((slots, 2, CHANS, LANES), jnp.float32),
            pltpu.VMEM((2 * LANES, 24 * LANES), jnp.bfloat16),
            pltpu.VMEM((2, 4 * LANES, LANES), jnp.bfloat16),
            pltpu.SMEM((slots,), jnp.int32),
            pltpu.SMEM((slots,), jnp.int32),
        ],
        in_specs=[smem, smem, vmem],
        out_specs=[vmem] * 3 + [smem] * 2,
        compiler_params=pltpu.CompilerParams(vmem_limit_bytes=SMALL_LIMIT),
        cost_estimate=pl.CostEstimate(flops=1_000_000, bytes_accessed=2_000_000, transcendentals=0),
    )(in_hbm(rows), in_hbm(cols), in_hbm(marker))


def descent_kernel(
    rows_ref,
    cols_ref,
    jones_ref,
    coher_hbm,
    seen_hbm,
    keep_ref,
    spread_ref,
    sums_ref,
    out_ref,
    coher_ref,
    seen_ref,
    wide_ref,
    left_ref,
    res_ref,
    row_ref,
    col_ref,
    coher_sem,
    seen_sem,
):
    slots = rows_ref.shape[0]
    blocks = jones_ref.shape[0]

    def copies(t):
        return (
            pltpu.make_async_copy(coher_hbm.at[t], coher_ref.at[t], coher_sem.at[t]),
            pltpu.make_async_copy(seen_hbm.at[t], seen_ref.at[t], seen_sem.at[t]),
        )

    for t in range(slots):
        for copy in copies(t):
            copy.start()
    out_ref[...] = jnp.zeros_like(out_ref)

    dense = jones_ref[...].reshape(blocks * DIRS * CHANS, LANES)
    high = dense.astype(jnp.bfloat16)
    low = (dense - high.astype(jnp.float32)).astype(jnp.bfloat16)
    split = jnp.concatenate([high, low], axis=1)
    for c in range(12):
        part = slice(256 * c, 256 * c + 256)
        wide = jnp.dot(split, spread_ref[:, part], preferred_element_type=jnp.float32)
        wide_ref[:, :, part] = wide.reshape(blocks * DIRS, CHANS, 256)

    def coher_of(t, k, half):
        kk, odd = k // 2, k % 2
        parts = []
        for e in range(8):
            block = coher_ref[t, e, 16 * kk : 16 * kk + 16, LANES * half : LANES * half + LANES]
            parts.append(block.astype(jnp.float32)[8 * odd : 8 * odd + 8])
        return pairs(parts)

    def expand(block, k, kind):
        return pairs(
            [
                wide_ref[block * DIRS + k, :, (3 * e + kind) * LANES : (3 * e + kind + 1) * LANES]
                for e in range(8)
            ]
        )

    lane = lane_iota()

    def merged(item, dist):
        low = (lane & dist) == 0
        kept = jnp.where(low, item[0], item[1])
        sent = jnp.where(low, item[1], item[0])
        if dist == LANES // 2:
            return kept + pltpu.roll(sent, dist, 1)
        return kept + jnp.take_along_axis(sent, lane ^ dist, axis=1, mode="promise_in_bounds")

    def put(ref, part, item):
        ref[0:8, part * LANES : part * LANES + LANES] = item[0]
        ref[8:16, part * LANES : part * LANES + LANES] = item[1]

    def multiply(t, carry):
        a = jnp.maximum(rows_ref[t], 0)
        b = jnp.maximum(cols_ref[t], 0)
        for copy in copies(t):
            copy.wait()

        @pl.when(rows_ref[t] >= 0)
        def _():
            accs = []
            for half in range(2):
                acc = []
                for e in range(4):
                    both = seen_ref[
                        t, 16 * e : 16 * e + 16, LANES * half : LANES * half + LANES
                    ].astype(jnp.float32)
                    acc.append((both[0:8], both[8:16]))
                accs.append(acc)
            for k in range(DIRS):
                right = expand(b, k, 0)
                for half in range(2):
                    left = mat_mul(expand(a, k, 1 + half), coher_of(t, k, half))
                    for e, piece in enumerate(flat(left)):
                        left_ref[half, k, e] = piece
                    accs[half] = mat_mul(left, right, accs[half], y_herm=True, minus=True)
            for half in range(2):
                keep = keep_ref[t, half]
                acc = with_sums([(item[0] * keep, item[1] * keep) for item in accs[half]])
                for e, piece in enumerate(flat(acc)):
                    res_ref[half, e] = piece
            for k in range(DIRS):
                right = with_sums(expand(b, k, 0))
                cols = [None] * 4
                for half in range(2):
                    res = [tuple(res_ref[half, 3 * e + n] for n in range(3)) for e in range(4)]
                    coher = coher_of(t, k, half)
                    turned = []
                    for i in range(2):
                        for j in range(2):
                            sums = conj_right(coher, right, (2 * i, 2 * i + 1), (2 * j, 2 * j + 1))
                            turned.append(conj_right_value(sums))
                    for e in range(4):
                        i, j = e // 2, e % 2
                        item = conj_left(turned, res, (2 * j, 2 * j + 1), (2 * i, 2 * i + 1))
                        put(row_ref.at[t, k, half], e, item)
                    left = pairs([left_ref[half, k, e] for e in range(8)])
                    for e in range(4):
                        i, j = e // 2, e % 2
                        cols[e] = conj_right(left, res, (j, 2 + j), (i, 2 + i), cols[e])
                        if half == 1:
                            col_ref[t, k, :, e * LANES : e * LANES + LANES] = merged(conj_right_value(cols[e]), 64)

        return carry

    lax.fori_loop(0, slots, multiply, 0)

    group = slots

    def total(values, sums):
        high = values.astype(jnp.bfloat16)
        low = values - high.astype(jnp.float32)
        out = jnp.dot(high, sums, preferred_element_type=jnp.float32)
        return out + jnp.dot(low, sums.astype(jnp.float32), preferred_element_type=jnp.float32)

    def settle(g, carry):
        t0 = g * group
        rows = total(row_ref[pl.ds(t0, group)].reshape(group * DIRS * 32, 4 * LANES), sums_ref[0])
        cols = total(col_ref[pl.ds(t0, group)].reshape(group * DIRS * 8, 4 * LANES), sums_ref[1])
        rows = rows.reshape(group, DIRS, 2, 2, CHANS, LANES)
        cols = cols.reshape(group, DIRS, CHANS, LANES)
        for n in range(group):
            a = jnp.maximum(rows_ref[t0 + n], 0)
            b = jnp.maximum(cols_ref[t0 + n], 0)
            live = rows_ref[t0 + n] >= 0
            for k in range(DIRS):
                row = [rows[n, k, 0, c] + pltpu.roll(rows[n, k, 1, c], 8, 1) for c in range(2)]
                row = row[0] + pltpu.roll(row[1], BLK, 1)
                out_ref[a, k] = out_ref[a, k] + jnp.where(live, row, 0.0)
            for k in range(DIRS):
                out_ref[b, k] = out_ref[b, k] + jnp.where(live, cols[n, k], 0.0)
        return carry

    lax.fori_loop(0, slots // group, settle, 0)


def local_descent(jones_full, rows, cols, coher, seen, staged):
    blocks = jones_full.shape[0]
    slots = rows.shape[0]
    vmem = pl.BlockSpec(memory_space=pltpu.VMEM)
    smem = pl.BlockSpec(memory_space=pltpu.SMEM)
    hbm = pl.BlockSpec(memory_space=pltpu.HBM)
    *staged, rows, cols = staged
    rows = pltpu.with_memory_space_constraint(rows, pltpu.SMEM)
    cols = pltpu.with_memory_space_constraint(cols, pltpu.SMEM)
    staged = [pltpu.with_memory_space_constraint(x, pltpu.VMEM) for x in staged]
    return pl.pallas_call(
        descent_kernel,
        out_shape=jax.ShapeDtypeStruct((blocks, DIRS, CHANS, LANES), jnp.float32),
        in_specs=[smem, smem, vmem, hbm, hbm] + [vmem] * 3,
        out_specs=vmem,
        scratch_shapes=[
            pltpu.VMEM(coher.shape, jnp.bfloat16),
            pltpu.VMEM(seen.shape, jnp.bfloat16),
            pltpu.VMEM((blocks * DIRS, CHANS, 24 * LANES), jnp.float32),
            pltpu.VMEM((2, DIRS, 8, CHANS, LANES), jnp.float32),
            pltpu.VMEM((2, 12, CHANS, LANES), jnp.float32),
            pltpu.VMEM((slots, DIRS, 2, 16, 4 * LANES), jnp.float32),
            pltpu.VMEM((slots, DIRS, CHANS, 4 * LANES), jnp.float32),
            pltpu.SemaphoreType.DMA((slots,)),
            pltpu.SemaphoreType.DMA((slots,)),
        ],
        compiler_params=pltpu.CompilerParams(vmem_limit_bytes=VMEM_LIMIT),
        cost_estimate=pl.CostEstimate(
            flops=40_000_000, bytes_accessed=4_000_000, transcendentals=0
        ),
    )(rows, cols, jones_full, in_hbm(coher), in_hbm(seen), *staged)


def sum_kernel(count, *refs):
    refs[-1][...] = sum([ref[...] for ref in refs[1:count]], refs[0][...])


def sum_of(parts, after=None):
    def body(*refs):
        sum_kernel(len(parts), *refs)

    waited = [] if after is None else [after]
    vmem = pl.BlockSpec(memory_space=pltpu.VMEM)
    return pl.pallas_call(
        body,
        out_shape=jax.ShapeDtypeStruct(parts[0].shape, parts[0].dtype),
        in_specs=[vmem] * len(parts) + [pl.BlockSpec(memory_space=pl.ANY)] * len(waited),
        out_specs=vmem,
        compiler_params=pltpu.CompilerParams(vmem_limit_bytes=SMALL_LIMIT),
    )(*parts, *waited)


def add_kernel(terms_ref, *refs):
    part_refs, (passed_ref, total_ref) = refs[:-2], refs[-2:]
    total_ref[...] = sum([ref[...] for ref in part_refs[1:]], part_refs[0][...])


def add_beside(terms, parts):
    vmem = pl.BlockSpec(memory_space=pltpu.VMEM)
    whole = pl.BlockSpec(memory_space=pl.ANY)
    return pl.pallas_call(
        add_kernel,
        out_shape=[
            jax.ShapeDtypeStruct(terms.shape, terms.dtype),
            jax.ShapeDtypeStruct(parts[0].shape, parts[0].dtype),
        ],
        in_specs=[whole] + [vmem] * len(parts),
        out_specs=[whole, vmem],
        input_output_aliases={0: 0},
        compiler_params=pltpu.CompilerParams(vmem_limit_bytes=SMALL_LIMIT),
    )(terms, *parts)


def to_dense_kernel(total, chan_ref, start_ref, dense_ref, sent_ref, part_ref):
    basis = basis_rows(chan_ref[0], total)
    for k in range(DIRS):
        field = jnp.concatenate([start_ref[e, k] for e in range(8)], axis=1)
        dense_ref[k] = field
        for n in range(sent_ref.shape[0]):
            sent_ref[n, k] = field
        part_ref[k] = jnp.concatenate(project_rows(field, basis), axis=0)


def descent_sum(terms_ref, k):
    parts = [terms_ref[n, k] for n in range(terms_ref.shape[0])]
    while len(parts) > 1:
        parts = [x + y for x, y in zip(parts[0::2], parts[1::2])]
    return parts[0]


def first_update_kernel(total, chan_ref, jones_ref, terms_ref, *refs):
    coeff_refs, (dense_ref, sent_ref, part_ref) = refs[:-3], refs[-3:]
    basis = basis_rows(chan_ref[0], total)
    for k in range(DIRS):
        coeffs = coeff_refs[0][k]
        for ref in coeff_refs[1:]:
            coeffs = coeffs + ref[k]
        now = jones_ref[k]
        now = now + MU * (
            descent_sum(terms_ref, k) / STATIONS - RHO * (now - expand_rows(coeffs, basis))
        )
        dense_ref[k] = now
        for n in range(sent_ref.shape[0]):
            sent_ref[n, k] = now
        part_ref[k] = jnp.concatenate(project_rows(now, basis), axis=0)


def second_sum_kernel(total, chan_ref, terms_ref, part_ref, descent_ref, sent_ref):
    basis = basis_rows(chan_ref[0], total)
    for k in range(DIRS):
        descent = descent_sum(terms_ref, k)
        descent_ref[k] = descent
        part = jnp.concatenate(
            [part_ref[k], jnp.concatenate(project_rows(descent, basis), axis=0)], axis=0
        )
        for n in range(sent_ref.shape[0]):
            sent_ref[n, k] = part


def finish_kernel(total, chan_ref, jones_ref, descent_ref, sums_ref, sol_ref, du_ref, co_ref):
    basis = basis_rows(chan_ref[0], total)
    for k in range(DIRS):
        both = descent_sum(sums_ref, k)
        coeffs = both[0:NP]
        now = jones_ref[k]
        dual = RHO * (now - expand_rows(coeffs, basis))
        now = now + MU * (descent_ref[k] / STATIONS - dual - dual)
        coeffs = coeffs + (MU / STATIONS) * both[NP : 2 * NP]
        dual = dual + RHO * (now - expand_rows(coeffs, basis))
        for e in range(8):
            part = slice(e * BLK, e * BLK + BLK)
            sol_ref[e, k] = now[:, part]
            du_ref[e, k] = dual[:, part]
            co_ref[e, k] = coeffs[:, part]


def small_call(kernel, total, chan, arrays, shapes):
    vmem = pl.BlockSpec(memory_space=pltpu.VMEM)
    smem = pl.BlockSpec(memory_space=pltpu.SMEM)

    def body(*refs):
        kernel(total, *refs)

    return pl.pallas_call(
        body,
        out_shape=[jax.ShapeDtypeStruct(s, jnp.float32) for s in shapes],
        in_specs=[smem] + [vmem] * len(arrays),
        out_specs=[vmem] * len(shapes),
        compiler_params=pltpu.CompilerParams(vmem_limit_bytes=SMALL_LIMIT),
    )(in_hbm(chan), *arrays)


def flipped(array, bits, count):
    return lax.ppermute(array, "chan", [(i, i ^ bits) for i in range(count)])


def exchanged(part, bits, count):
    masks = [0]
    for bit in bits:
        masks += [m ^ bit for m in masks]
    return [part] + [flipped(part, m, count) for m in masks[1:]]


def local(start, coher, seen, marker, rows, cols):
    pair_count = lax.axis_size("pair")
    chan_count = lax.axis_size("chan")
    total = CHANS * chan_count
    chan = lax.axis_index("chan").astype(jnp.int32).reshape(1)
    coher = coher.reshape(coher.shape[0], 8, DIRS * CHANS, BLK * BLK)
    seen = seen.reshape(seen.shape[0], 8 * CHANS, BLK * BLK)
    block = (DIRS, CHANS, LANES)
    blocks = (pair_count,) + block
    poly = (DIRS, NP, LANES)
    jones, sent, part = small_call(to_dense_kernel, total, chan, [in_hbm(start)], [block, blocks, poly])
    full = lax.all_to_all(sent, "pair", 0, 0)
    bits = [1 << i for i in range(chan_count.bit_length() - 1)]
    part = sum_of(exchanged(part, bits[:1], chan_count))
    staged = stage(marker, rows, cols)
    part = sum_of(exchanged(part, bits[1:3], chan_count), after=staged[0])
    terms = local_descent(full, rows, cols, coher, seen, staged)
    terms, coeffs = add_beside(terms, exchanged(part, bits[3:], chan_count))
    terms = lax.all_to_all(terms, "pair", 0, 0)
    jones, sent, part = small_call(
        first_update_kernel, total, chan, [jones, terms, coeffs], [block, blocks, poly]
    )
    full = lax.all_to_all(sent, "pair", 0, 0)
    terms = local_descent(full, rows, cols, coher, seen, staged)
    terms = lax.all_to_all(terms, "pair", 0, 0)
    descent, sums = small_call(
        second_sum_kernel,
        total,
        chan,
        [terms, part],
        [block, (chan_count, DIRS, 2 * NP, LANES)],
    )
    sums = lax.all_to_all(sums, "chan", 0, 0)
    return small_call(
        finish_kernel,
        total,
        chan,
        [jones, descent, sums],
        [(8, DIRS, CHANS, BLK), (8, DIRS, CHANS, BLK), (8, DIRS, NP, BLK)],
    )


def solution(mesh):
    placed = (
        P(None, None, "chan", "pair"),
        P("pair", None, None, "chan", None),
        P("pair", None, "chan", None),
        P("pair", None),
        P("pair"),
        P("pair"),
    )
    return jax.shard_map(
        local,
        mesh=mesh,
        in_specs=placed,
        out_specs=(
            P(None, None, "chan", "pair"),
            P(None, None, "chan", "pair"),
            P(None, None, None, "pair"),
        ),
        check_vma=False,
    )
```

```python
import math

import jax
import jax.numpy as jnp
from jax import lax
from jax.experimental import pallas as pl
from jax.experimental.pallas import tpu as pltpu
from jax.sharding import PartitionSpec as P

STATIONS = 256
BLK = 16
NP = 4
RHO = 0.5
MU = 1.0
LANES = 128
CHANS = 8
DIRS = 4
VMEM_LIMIT = 32 * 1024 * 1024
SMALL_LIMIT = 8 * 1024 * 1024


def in_hbm(array):
    return pltpu.with_memory_space_constraint(array, pltpu.HBM)


def lane_iota():
    return lax.broadcasted_iota(jnp.int32, (CHANS, LANES), 1)


def basis_rows(chan, total):
    freq = (chan * CHANS + lax.broadcasted_iota(jnp.int32, (CHANS, LANES), 0)).astype(jnp.float32)
    rows = [jnp.full((CHANS, LANES), math.sqrt(1.0 / total), jnp.float32)]
    for m in range(1, NP):
        rows.append(math.sqrt(2.0 / total) * jnp.cos((math.pi * m) * (freq + 0.5) / total))
    return rows


def project_rows(field, basis):
    return [jnp.sum(basis[m] * field, axis=0, keepdims=True) for m in range(NP)]


def expand_rows(coeffs, basis):
    total = basis[0] * coeffs[0:1]
    for m in range(1, NP):
        total = total + basis[m] * coeffs[m : m + 1]
    return total


def acc_mul(acc, a, b, conj_a=False, conj_b=False, minus=False):
    rr, ii = a[0] * b[0], a[1] * b[1]
    ri, ir = a[0] * b[1], a[1] * b[0]
    sign_ii = -1 if conj_a == conj_b else 1
    sign_ri = -1 if conj_b else 1
    sign_ir = -1 if conj_a else 1
    if minus:
        sign_ii, sign_ri, sign_ir = -sign_ii, -sign_ri, -sign_ir
    sign_rr = -1 if minus else 1

    def put(base, value, sign):
        if base is None:
            return value if sign > 0 else -value
        return base + value if sign > 0 else base - value

    if acc is None:
        real = rr + ii if sign_ii == sign_rr else rr - ii
        if sign_ri == sign_ir:
            imag = ri + ir
        else:
            imag = ri - ir if sign_ri > 0 else ir - ri
        if minus:
            raise ValueError
        return (real, imag)
    return (
        put(put(acc[0], rr, sign_rr), ii, sign_ii),
        put(put(acc[1], ri, sign_ri), ir, sign_ir),
    )


def mat_mul(x, y, acc=None, x_herm=False, y_herm=False, minus=False):
    out = []
    for i in range(2):
        for j in range(2):
            item = None if acc is None else acc[2 * i + j]
            for l in range(2):
                left = x[2 * l + i] if x_herm else x[2 * i + l]
                right = y[2 * j + l] if y_herm else y[2 * l + j]
                item = acc_mul(item, left, right, x_herm, y_herm, minus)
            out.append(item)
    return out


def mat_entry(x, y, i, j, item=None, x_herm=False, y_herm=False):
    for l in range(2):
        left = x[2 * l + i] if x_herm else x[2 * i + l]
        right = y[2 * j + l] if y_herm else y[2 * l + j]
        item = acc_mul(item, left, right, x_herm, y_herm)
    return item


def with_sums(matrix):
    return [(item[0], item[1] - item[0], item[0] + item[1]) for item in matrix]


def three(sums, first, second, third):
    terms = (first[0] * first[1], second[0] * second[1], third[0] * third[1])
    return terms if sums is None else tuple(x + y for x, y in zip(sums, terms))


def conj_right(x, y, left, right, sums=None):
    for l, r in zip(left, right):
        re, im = x[l]
        sums = three(sums, (y[r][0], re + im), (im, y[r][1]), (re, y[r][2]))
    return sums


def conj_right_value(sums):
    return (sums[0] + sums[1], sums[0] - sums[2])


def conj_left(x, y, left, right):
    sums = None
    for l, r in zip(left, right):
        re, im = x[l]
        sums = three(sums, (y[r][0], re - im), (im, y[r][2]), (re, y[r][1]))
    return (sums[0] + sums[1], sums[0] + sums[2])


def pairs(list8):
    return [(list8[2 * e], list8[2 * e + 1]) for e in range(4)]


def flat(matrix):
    return [piece for item in matrix for piece in item]


def one_hot(hit):
    return jnp.where(hit, 1.0, 0.0).astype(jnp.bfloat16)


def stage_kernel(
    rows_ref, cols_ref, marker_ref, keep_ref, spread_ref, sums_ref, rows_out, cols_out
):
    for t in range(rows_ref.shape[0]):
        rows_out[t] = rows_ref[t]
        cols_out[t] = cols_ref[t]
    source = lax.broadcasted_iota(jnp.int32, (LANES, LANES), 0)
    target = lax.broadcasted_iota(jnp.int32, (LANES, LANES), 1)
    tables = [target % BLK, target // BLK, target // BLK + 8]
    for n in range(24):
        one = one_hot(source == (n // 3) * BLK + tables[n % 3])
        spread_ref[0:LANES, n * LANES : n * LANES + LANES] = one
        spread_ref[LANES : 2 * LANES, n * LANES : n * LANES + LANES] = one
    column = source // 64 * BLK + source % BLK
    for n in range(4):
        sums_ref[0, n * LANES : n * LANES + LANES] = one_hot(target == 2 * n * BLK + source // BLK)
        sums_ref[1, n * LANES : n * LANES + LANES] = one_hot(target == 2 * n * BLK + column)

    lane = lane_iota()
    for t in range(rows_ref.shape[0]):
        for half in range(2):
            mark = marker_ref[t : t + 1, LANES * half : LANES * half + LANES].astype(jnp.float32)
            keep = jnp.broadcast_to(mark, (CHANS, LANES))
            off_diagonal = rows_ref[t] != cols_ref[t]
            upper = lane // BLK + 8 * half < lane % BLK
            keep = jnp.where((off_diagonal | upper) & (rows_ref[t] >= 0), keep, 0.0)
            keep_ref[t, half] = keep


def stage(marker, rows, cols):
    slots = rows.shape[0]
    vmem = pl.BlockSpec(memory_space=pltpu.VMEM)
    smem = pl.BlockSpec(memory_space=pltpu.SMEM)
    return pl.pallas_call(
        stage_kernel,
        out_shape=[
            pltpu.VMEM((slots, 2, CHANS, LANES), jnp.float32),
            pltpu.VMEM((2 * LANES, 24 * LANES), jnp.bfloat16),
            pltpu.VMEM((2, 4 * LANES, LANES), jnp.bfloat16),
            pltpu.SMEM((slots,), jnp.int32),
            pltpu.SMEM((slots,), jnp.int32),
        ],
        in_specs=[smem, smem, vmem],
        out_specs=[vmem] * 3 + [smem] * 2,
        compiler_params=pltpu.CompilerParams(vmem_limit_bytes=SMALL_LIMIT),
        cost_estimate=pl.CostEstimate(flops=1_000_000, bytes_accessed=2_000_000, transcendentals=0),
    )(in_hbm(rows), in_hbm(cols), in_hbm(marker))


def descent_kernel(
    rows_ref,
    cols_ref,
    jones_ref,
    coher_hbm,
    seen_hbm,
    keep_ref,
    spread_ref,
    sums_ref,
    out_ref,
    coher_ref,
    seen_ref,
    wide_ref,
    left_ref,
    res_ref,
    row_ref,
    col_ref,
    coher_sem,
    seen_sem,
):
    slots = rows_ref.shape[0]
    blocks = jones_ref.shape[0]

    def copies(t):
        return (
            pltpu.make_async_copy(coher_hbm.at[t], coher_ref.at[t], coher_sem.at[t]),
            pltpu.make_async_copy(seen_hbm.at[t], seen_ref.at[t], seen_sem.at[t]),
        )

    for t in range(slots):
        for copy in copies(t):
            copy.start()
    out_ref[...] = jnp.zeros_like(out_ref)

    dense = jones_ref[...].reshape(blocks * DIRS * CHANS, LANES)
    high = dense.astype(jnp.bfloat16)
    low = (dense - high.astype(jnp.float32)).astype(jnp.bfloat16)
    split = jnp.concatenate([high, low], axis=1)
    for c in range(12):
        part = slice(256 * c, 256 * c + 256)
        wide = jnp.dot(split, spread_ref[:, part], preferred_element_type=jnp.float32)
        wide_ref[:, :, part] = wide.reshape(blocks * DIRS, CHANS, 256)

    def coher_of(t, k, half):
        kk, odd = k // 2, k % 2
        parts = []
        for e in range(8):
            block = coher_ref[t, e, 16 * kk : 16 * kk + 16, LANES * half : LANES * half + LANES]
            parts.append(block.astype(jnp.float32)[8 * odd : 8 * odd + 8])
        return pairs(parts)

    def expand(block, k, kind):
        return pairs(
            [
                wide_ref[block * DIRS + k, :, (3 * e + kind) * LANES : (3 * e + kind + 1) * LANES]
                for e in range(8)
            ]
        )

    lane = lane_iota()

    def merged(item, dist):
        low = (lane & dist) == 0
        kept = jnp.where(low, item[0], item[1])
        sent = jnp.where(low, item[1], item[0])
        if dist == LANES // 2:
            return kept + pltpu.roll(sent, dist, 1)
        return kept + jnp.take_along_axis(sent, lane ^ dist, axis=1, mode="promise_in_bounds")

    def put(ref, part, item):
        ref[0:8, part * LANES : part * LANES + LANES] = item[0]
        ref[8:16, part * LANES : part * LANES + LANES] = item[1]

    def multiply(t, carry):
        a = jnp.maximum(rows_ref[t], 0)
        b = jnp.maximum(cols_ref[t], 0)
        for copy in copies(t):
            copy.wait()

        @pl.when(rows_ref[t] >= 0)
        def _():
            accs = []
            for half in range(2):
                acc = []
                for e in range(4):
                    both = seen_ref[
                        t, 16 * e : 16 * e + 16, LANES * half : LANES * half + LANES
                    ].astype(jnp.float32)
                    acc.append((both[0:8], both[8:16]))
                accs.append(acc)
            for k in range(DIRS):
                right = expand(b, k, 0)
                for half in range(2):
                    left = mat_mul(expand(a, k, 1 + half), coher_of(t, k, half))
                    for e, piece in enumerate(flat(left)):
                        left_ref[half, k, e] = piece
                    accs[half] = mat_mul(left, right, accs[half], y_herm=True, minus=True)
            for half in range(2):
                keep = keep_ref[t, half]
                acc = with_sums([(item[0] * keep, item[1] * keep) for item in accs[half]])
                for e, piece in enumerate(flat(acc)):
                    res_ref[half, e] = piece
            for k in range(DIRS):
                right = with_sums(expand(b, k, 0))
                cols = [None] * 4
                for half in range(2):
                    res = [tuple(res_ref[half, 3 * e + n] for n in range(3)) for e in range(4)]
                    coher = coher_of(t, k, half)
                    turned = []
                    for i in range(2):
                        for j in range(2):
                            sums = conj_right(coher, right, (2 * i, 2 * i + 1), (2 * j, 2 * j + 1))
                            turned.append(conj_right_value(sums))
                    for e in range(4):
                        i, j = e // 2, e % 2
                        item = conj_left(turned, res, (2 * j, 2 * j + 1), (2 * i, 2 * i + 1))
                        put(row_ref.at[t, k, half], e, item)
                    left = pairs([left_ref[half, k, e] for e in range(8)])
                    for e in range(4):
                        i, j = e // 2, e % 2
                        cols[e] = conj_right(left, res, (j, 2 + j), (i, 2 + i), cols[e])
                        if half == 1:
                            col_ref[t, k, :, e * LANES : e * LANES + LANES] = merged(conj_right_value(cols[e]), 64)

        return carry

    lax.fori_loop(0, slots, multiply, 0)

    group = slots

    def total(values, sums):
        high = values.astype(jnp.bfloat16)
        low = values - high.astype(jnp.float32)
        out = jnp.dot(high, sums, preferred_element_type=jnp.float32)
        return out + jnp.dot(low, sums.astype(jnp.float32), preferred_element_type=jnp.float32)

    def settle(g, carry):
        t0 = g * group
        rows = total(row_ref[pl.ds(t0, group)].reshape(group * DIRS * 32, 4 * LANES), sums_ref[0])
        cols = total(col_ref[pl.ds(t0, group)].reshape(group * DIRS * 8, 4 * LANES), sums_ref[1])
        rows = rows.reshape(group, DIRS, 2, 2, CHANS, LANES)
        cols = cols.reshape(group, DIRS, CHANS, LANES)
        for n in range(group):
            a = jnp.maximum(rows_ref[t0 + n], 0)
            b = jnp.maximum(cols_ref[t0 + n], 0)
            live = rows_ref[t0 + n] >= 0
            for k in range(DIRS):
                row = [rows[n, k, 0, c] + pltpu.roll(rows[n, k, 1, c], 8, 1) for c in range(2)]
                row = row[0] + pltpu.roll(row[1], BLK, 1)
                out_ref[a, k] = out_ref[a, k] + jnp.where(live, row, 0.0)
            for k in range(DIRS):
                out_ref[b, k] = out_ref[b, k] + jnp.where(live, cols[n, k], 0.0)
        return carry

    lax.fori_loop(0, slots // group, settle, 0)


def local_descent(jones_full, rows, cols, coher, seen, staged):
    blocks = jones_full.shape[0]
    slots = rows.shape[0]
    vmem = pl.BlockSpec(memory_space=pltpu.VMEM)
    smem = pl.BlockSpec(memory_space=pltpu.SMEM)
    hbm = pl.BlockSpec(memory_space=pltpu.HBM)
    *staged, rows, cols = staged
    rows = pltpu.with_memory_space_constraint(rows, pltpu.SMEM)
    cols = pltpu.with_memory_space_constraint(cols, pltpu.SMEM)
    staged = [pltpu.with_memory_space_constraint(x, pltpu.VMEM) for x in staged]
    return pl.pallas_call(
        descent_kernel,
        out_shape=jax.ShapeDtypeStruct((blocks, DIRS, CHANS, LANES), jnp.float32),
        in_specs=[smem, smem, vmem, hbm, hbm] + [vmem] * 3,
        out_specs=vmem,
        scratch_shapes=[
            pltpu.VMEM(coher.shape, jnp.bfloat16),
            pltpu.VMEM(seen.shape, jnp.bfloat16),
            pltpu.VMEM((blocks * DIRS, CHANS, 24 * LANES), jnp.float32),
            pltpu.VMEM((2, DIRS, 8, CHANS, LANES), jnp.float32),
            pltpu.VMEM((2, 12, CHANS, LANES), jnp.float32),
            pltpu.VMEM((slots, DIRS, 2, 16, 4 * LANES), jnp.float32),
            pltpu.VMEM((slots, DIRS, CHANS, 4 * LANES), jnp.float32),
            pltpu.SemaphoreType.DMA((slots,)),
            pltpu.SemaphoreType.DMA((slots,)),
        ],
        compiler_params=pltpu.CompilerParams(vmem_limit_bytes=VMEM_LIMIT),
        cost_estimate=pl.CostEstimate(
            flops=40_000_000, bytes_accessed=4_000_000, transcendentals=0
        ),
    )(rows, cols, jones_full, in_hbm(coher), in_hbm(seen), *staged)


def sum_kernel(count, *refs):
    refs[-1][...] = sum([ref[...] for ref in refs[1:count]], refs[0][...])


def sum_of(parts, after=None):
    def body(*refs):
        sum_kernel(len(parts), *refs)

    waited = [] if after is None else [after]
    vmem = pl.BlockSpec(memory_space=pltpu.VMEM)
    return pl.pallas_call(
        body,
        out_shape=jax.ShapeDtypeStruct(parts[0].shape, parts[0].dtype),
        in_specs=[vmem] * len(parts) + [pl.BlockSpec(memory_space=pl.ANY)] * len(waited),
        out_specs=vmem,
        compiler_params=pltpu.CompilerParams(vmem_limit_bytes=SMALL_LIMIT),
    )(*parts, *waited)


def add_kernel(terms_ref, *refs):
    part_refs, (passed_ref, total_ref) = refs[:-2], refs[-2:]
    total_ref[...] = sum([ref[...] for ref in part_refs[1:]], part_refs[0][...])


def add_beside(terms, parts):
    vmem = pl.BlockSpec(memory_space=pltpu.VMEM)
    whole = pl.BlockSpec(memory_space=pl.ANY)
    return pl.pallas_call(
        add_kernel,
        out_shape=[
            jax.ShapeDtypeStruct(terms.shape, terms.dtype),
            jax.ShapeDtypeStruct(parts[0].shape, parts[0].dtype),
        ],
        in_specs=[whole] + [vmem] * len(parts),
        out_specs=[whole, vmem],
        input_output_aliases={0: 0},
        compiler_params=pltpu.CompilerParams(vmem_limit_bytes=SMALL_LIMIT),
    )(terms, *parts)


def to_dense_kernel(total, chan_ref, start_ref, dense_ref, sent_ref, part_ref):
    basis = basis_rows(chan_ref[0], total)
    for k in range(DIRS):
        field = jnp.concatenate([start_ref[e, k] for e in range(8)], axis=1)
        dense_ref[k] = field
        for n in range(sent_ref.shape[0]):
            sent_ref[n, k] = field
        part_ref[k] = jnp.concatenate(project_rows(field, basis), axis=0)


def descent_sum(terms_ref, k):
    parts = [terms_ref[n, k] for n in range(terms_ref.shape[0])]
    while len(parts) > 1:
        parts = [x + y for x, y in zip(parts[0::2], parts[1::2])]
    return parts[0]


def first_update_kernel(total, chan_ref, jones_ref, terms_ref, *refs):
    coeff_refs, (dense_ref, sent_ref, part_ref) = refs[:-3], refs[-3:]
    basis = basis_rows(chan_ref[0], total)
    for k in range(DIRS):
        coeffs = coeff_refs[0][k]
        for ref in coeff_refs[1:]:
            coeffs = coeffs + ref[k]
        now = jones_ref[k]
        now = now + MU * (
            descent_sum(terms_ref, k) / STATIONS - RHO * (now - expand_rows(coeffs, basis))
        )
        dense_ref[k] = now
        for n in range(sent_ref.shape[0]):
            sent_ref[n, k] = now
        part_ref[k] = jnp.concatenate(project_rows(now, basis), axis=0)


def second_sum_kernel(total, chan_ref, terms_ref, part_ref, descent_ref, sent_ref):
    basis = basis_rows(chan_ref[0], total)
    for k in range(DIRS):
        descent = descent_sum(terms_ref, k)
        descent_ref[k] = descent
        part = jnp.concatenate(
            [part_ref[k], jnp.concatenate(project_rows(descent, basis), axis=0)], axis=0
        )
        for n in range(sent_ref.shape[0]):
            sent_ref[n, k] = part


def finish_kernel(total, chan_ref, jones_ref, descent_ref, sums_ref, sol_ref, du_ref, co_ref):
    basis = basis_rows(chan_ref[0], total)
    held = []
    for k in range(DIRS):
        both = descent_sum(sums_ref, k)
        coeffs = both[0:NP]
        now = jones_ref[k]
        dual = RHO * (now - expand_rows(coeffs, basis))
        now = now + MU * (descent_ref[k] / STATIONS - dual - dual)
        coeffs = coeffs + (MU / STATIONS) * both[NP : 2 * NP]
        dual = dual + RHO * (now - expand_rows(coeffs, basis))
        for e in range(8):
            part = slice(e * BLK, e * BLK + BLK)
            sol_ref[e, k] = now[:, part]
            du_ref[e, k] = dual[:, part]
        held.append(coeffs)
    for k in range(0, DIRS, 2):
        two = jnp.concatenate(held[k : k + 2], axis=0)
        for e in range(8):
            part = two[:, e * BLK : e * BLK + BLK]
            co_ref[e, k] = part[0:NP]
            co_ref[e, k + 1] = part[NP : 2 * NP]


def small_call(kernel, total, chan, arrays, shapes):
    vmem = pl.BlockSpec(memory_space=pltpu.VMEM)
    smem = pl.BlockSpec(memory_space=pltpu.SMEM)

    def body(*refs):
        kernel(total, *refs)

    return pl.pallas_call(
        body,
        out_shape=[jax.ShapeDtypeStruct(s, jnp.float32) for s in shapes],
        in_specs=[smem] + [vmem] * len(arrays),
        out_specs=[vmem] * len(shapes),
        compiler_params=pltpu.CompilerParams(vmem_limit_bytes=SMALL_LIMIT),
    )(in_hbm(chan), *arrays)


def flipped(array, bits, count):
    return lax.ppermute(array, "chan", [(i, i ^ bits) for i in range(count)])


def exchanged(part, bits, count):
    masks = [0]
    for bit in bits:
        masks += [m ^ bit for m in masks]
    return [part] + [flipped(part, m, count) for m in masks[1:]]


def local(start, coher, seen, marker, rows, cols):
    pair_count = lax.axis_size("pair")
    chan_count = lax.axis_size("chan")
    total = CHANS * chan_count
    chan = lax.axis_index("chan").astype(jnp.int32).reshape(1)
    coher = coher.reshape(coher.shape[0], 8, DIRS * CHANS, BLK * BLK)
    seen = seen.reshape(seen.shape[0], 8 * CHANS, BLK * BLK)
    block = (DIRS, CHANS, LANES)
    blocks = (pair_count,) + block
    poly = (DIRS, NP, LANES)
    jones, sent, part = small_call(to_dense_kernel, total, chan, [in_hbm(start)], [block, blocks, poly])
    full = lax.all_to_all(sent, "pair", 0, 0)
    bits = [1 << i for i in range(chan_count.bit_length() - 1)]
    part = sum_of(exchanged(part, bits[:1], chan_count))
    staged = stage(marker, rows, cols)
    part = sum_of(exchanged(part, bits[1:3], chan_count), after=staged[0])
    terms = local_descent(full, rows, cols, coher, seen, staged)
    terms, coeffs = add_beside(terms, exchanged(part, bits[3:], chan_count))
    terms = lax.all_to_all(terms, "pair", 0, 0)
    jones, sent, part = small_call(
        first_update_kernel, total, chan, [jones, terms, coeffs], [block, blocks, poly]
    )
    full = lax.all_to_all(sent, "pair", 0, 0)
    terms = local_descent(full, rows, cols, coher, seen, staged)
    terms = lax.all_to_all(terms, "pair", 0, 0)
    descent, sums = small_call(
        second_sum_kernel,
        total,
        chan,
        [terms, part],
        [block, (chan_count, DIRS, 2 * NP, LANES)],
    )
    sums = lax.all_to_all(sums, "chan", 0, 0)
    return small_call(
        finish_kernel,
        total,
        chan,
        [jones, descent, sums],
        [(8, DIRS, CHANS, BLK), (8, DIRS, CHANS, BLK), (8, DIRS, NP, BLK)],
    )


def solution(mesh):
    placed = (
        P(None, None, "chan", "pair"),
        P("pair", None, None, "chan", None),
        P("pair", None, "chan", None),
        P("pair", None),
        P("pair"),
        P("pair"),
    )
    return jax.shard_map(
        local,
        mesh=mesh,
        in_specs=placed,
        out_specs=(
            P(None, None, "chan", "pair"),
            P(None, None, "chan", "pair"),
            P(None, None, None, "pair"),
        ),
        check_vma=False,
    )
```
